32 devices in a mesh: xline: 4 (over y, x), inline: 8 (over z, core).
Axes of the slice: x: 2, y: 2, z: 4, core: 2. Of those that a mesh axis runs over, the one named last changes fastest.
Arguments:
- pressure: float32 [256, 256, 256], P('inline', 'xline'), may hold values from -6 to 6
- vel_inline: float32 [256, 256, 256], P('inline', 'xline'), may hold values from -6 to 6
- vel_xline: float32 [256, 256, 256], P('inline', 'xline'), may hold values from -6 to 6
- vel_depth: float32 [256, 256, 256], P('inline', 'xline'), may hold values from -6 to 6
- modulus: float32 [256, 256, 256], P('inline', 'xline'), may hold values from 0.5 to 1.5
- buoyancy: float32 [256, 256, 256], P('inline', 'xline'), may hold values from 0.5 to 1.5
- traces: float32 [24576, 512], P(('xline', 'inline')), may hold values from -6 to 6
- owner: int32 [24576, 1], P(('xline', 'inline')), may hold values from 0 to 31; in each aligned block of 768 rows (0 to 767, 768 to 1535, ...) at most 60 rows name the same one
- node_cell: int32 [24576], P(('xline', 'inline')), may hold values from 0 to 524287
- resample: float32 [4, 512], replicated, may hold values from -0.25 to 0.25
Outputs:
- pressure_out: float32 [256, 256, 256], P('inline', 'xline')
- inline_out: float32 [256, 256, 256], P('inline', 'xline')
- xline_out: float32 [256, 256, 256], P('inline', 'xline')
- depth_out: float32 [256, 256, 256], P('inline', 'xline')
The draws below stay inside these ranges and needn't reach their ends.
Inputs may be any that keep to these rules, and one draw needn't show every extreme that they name: Among the nodes of one device, at most 60 have the same owner.
All inputs are finite; a program needn't handle non-finite values.
Results may differ from the reference program's by a relative error of at most 0.0002.
Values sent between devices are 32-bit elements; how exact they have to be, the bound alone decides.
No kernel may reach another device: no remote copies, remote signals or barrier semaphores. Data moves between devices by JAX's collectives and lax.ppermute only.
A program may use at most 128 MiB of HBM per device.

```python
import math
import jax
import jax.numpy as jnp
import numpy as np
from jax import lax

CI = 32
CX = 64
NZ = 256
STEPS = 4
SAMPLES = 512
TRACE_DEV = 768
NI = 256
NX = 256
NODES = 24576
CAP = 60
N_INLINE = 8
DEVICES = 32


def set_ends(entries, own_key, least, top_value):
    place = [jax.random.randint(jax.random.fold_in(own_key, axis), (), 0, length) for axis, length in enumerate(entries.shape)]
    longest = entries.shape.index(max(entries.shape))
    next_to = place[:longest] + [(place[longest] + 1) % entries.shape[longest]] + place[longest + 1:]
    return entries.at[tuple(place)].set(least).at[tuple(next_to)].set(top_value)


def levels(rng, shape, split, smallest, high):
    level = 1.0
    for position, blocks in split:
        draws = jax.random.uniform(jax.random.fold_in(jax.random.fold_in(rng, 6), position), (blocks,), jnp.float32, smallest / len(split), high / len(split))
        level = level * jnp.repeat(jnp.exp(draws), shape[position] // blocks).reshape((-1,) + (1,) * (len(shape) - 1 - position))
    return level


def deal_out(key, own, number, rows, number_of, top, reach, slope):
    order = jax.random.permutation(key, number_of)
    heavy_load, ordinary = load_shares(number_of, rows * top, reach, slope, True), load_shares(number_of, rows * top, reach, slope, False)
    places = jnp.arange(number_of)

    def named(tallies, rotation):
        used = int((tallies > 0).sum())
        fixed = max(1, used // 4)
        shifted = fixed + (places - fixed + rotation * (used - fixed)) % max(1, number_of - fixed)
        return jnp.zeros((number_of,), jnp.int32).at[order[jnp.where(places < fixed, places, shifted)]].set(jnp.asarray(tallies, jnp.int32))

    tallies = jnp.where(number % 4 == 0, named(heavy_load, number // 4), named(ordinary, number - number // 4 - 1))
    mixed = jax.random.permutation(jax.random.fold_in(own, 3), number_of)
    donor, sink = mixed[0:number_of // 2 * 2:2], mixed[1:number_of // 2 * 2:2]
    slack = jnp.minimum(tallies[donor] - 1, reach - tallies[sink]) // 2
    slack = jnp.where((donor == order[0]) | (sink == order[0]) | (tallies[sink] == 0), 0, jnp.maximum(slack, 0))
    shifted = jax.random.randint(jax.random.fold_in(own, 4), (number_of // 2,), 0, 1 << 20) % (slack + 1)
    tallies = tallies.at[donor].add(-shifted).at[sink].add(shifted)
    items = jnp.searchsorted(jnp.cumsum(tallies), jnp.arange(rows * top), side="right").astype(jnp.int32)
    listing = items.reshape(top, rows).T
    listing = listing[jax.random.permutation(jax.random.fold_in(own, 1), rows)]
    rotation = jax.random.randint(jax.random.fold_in(own, 2), (rows, 1), 0, top)
    return jnp.take_along_axis(listing, (jnp.arange(top)[None, :] + rotation) % top, axis=1)


def load_shares(count, total, bound, skew, full):
    weights = [(1 << 20) // math.isqrt(grade ** skew) + 1 for grade in range(1, count + 1)]
    largest = bound if full else min(bound, max(-(-total // count), total * weights[0] // sum(weights)))
    least = 1 if total - largest >= count - 1 else 0
    holding, rest = [largest] + [least] * (count - 1), total - largest - least * (count - 1)
    while rest > 0:
        candidates = [i for i in range(1, count) if holding[i] < largest] or [i for i in range(1, count) if holding[i] < bound]
        pool, left = sum([weights[i] for i in candidates]), rest
        for i in candidates:
            extra = min(bound - holding[i], max(1, left * weights[i] // pool), rest)
            holding[i] = holding[i] + extra
            rest = rest - extra
    return np.array(holding)


def normal_values(rng, dims, scale, bound, shards=(), dtype=jnp.bfloat16):
    level = levels(rng, dims, shards, -0.22, 0.18) if shards else 1.0
    values = jax.random.normal(rng, dims, jnp.float32) * scale * level
    return jnp.minimum(jnp.maximum(values, -bound), bound).astype(dtype)


def setup_inputs(seed: int = 0) -> dict:
    seeds = jax.random.split(jax.random.key(seed), 11)
    pressure = normal_values(seeds[0], (NI, NX, NZ), 1.0, 6.0, ((0, 8), (1, 4)), jnp.float32)
    vel_inline = normal_values(seeds[1], (NI, NX, NZ), 1.0, 6.0, ((0, 8), (1, 4)), jnp.float32)
    vel_xline = normal_values(seeds[2], (NI, NX, NZ), 1.0, 6.0, ((0, 8), (1, 4)), jnp.float32)
    vel_depth = normal_values(seeds[3], (NI, NX, NZ), 1.0, 6.0, ((0, 8), (1, 4)), jnp.float32)
    modulus = jnp.clip(jnp.exp(math.log(1.5) - 1.0986123 * jax.random.uniform(seeds[4], (NI, NX, NZ), jnp.float32) ** levels(seeds[4], (NI, NX, NZ), ((0, 8), (1, 4)), -0.2, 0.2)), 0.5, 1.5)
    buoyancy = jnp.clip(jnp.exp(math.log(1.5) - 1.0986123 * jax.random.uniform(seeds[5], (NI, NX, NZ), jnp.float32) ** levels(seeds[5], (NI, NX, NZ), ((0, 8), (1, 4)), -0.2, 0.2)), 0.5, 1.5)
    traces = normal_values(seeds[6], (NODES, SAMPLES), 1.0, 6.0, ((0, 32),), jnp.float32)
    owner_keys = jax.random.split(jax.random.fold_in(seeds[7], 1), NODES // TRACE_DEV)
    owner_turns = jax.random.permutation(jax.random.fold_in(seeds[7], 3), NODES // TRACE_DEV)
    owner = jax.vmap(lambda own, number: deal_out(jax.random.fold_in(seeds[7], 2), own, number, TRACE_DEV, DEVICES, 1, CAP, 2))(owner_keys, owner_turns).reshape((NODES, 1))
    node_cell = set_ends(jax.random.randint(seeds[8], (NODES,), 0, CI * CX * NZ), jax.random.fold_in(seeds[8], 1), 0, (CI * CX * NZ) - 1).astype(jnp.int32)
    resample = normal_values(seeds[9], (STEPS, SAMPLES), SAMPLES ** -0.5, 0.25, (), jnp.float32)
    return dict(pressure=pressure, vel_inline=vel_inline, vel_xline=vel_xline, vel_depth=vel_depth, modulus=modulus, buoyancy=buoyancy, traces=traces, owner=owner, node_cell=node_cell, resample=resample)


COURANT = 0.35


def reference(pressure, vel_inline, vel_xline, vel_depth, modulus, buoyancy, traces, owner, node_cell, resample):
    sources = jnp.dot(traces, resample.T, precision=lax.Precision.HIGHEST, preferred_element_type=jnp.float32)
    owner_id = owner[:, 0].astype(jnp.int32)
    xline_block = owner_id // N_INLINE
    inline_block = owner_id % N_INLINE
    row_index = inline_block * CI + node_cell // (CX * NZ)
    column_index = xline_block * CX + (node_cell // NZ) % CX
    depth_index = node_cell % NZ
    targets = ((row_index * NX + column_index) * NZ + depth_index).astype(jnp.int32)
    weights = COURANT * modulus.reshape(-1)[targets]
    field_shape = pressure.shape
    for step_index in range(STEPS):
        zero_row = jnp.zeros((1, field_shape[1], field_shape[2]), jnp.float32)
        zero_col = jnp.zeros((field_shape[0], 1, field_shape[2]), jnp.float32)
        zero_dep = jnp.zeros((field_shape[0], field_shape[1], 1), jnp.float32)
        grad_inline = jnp.concatenate([pressure[1:], zero_row], 0) - pressure
        grad_xline = jnp.concatenate([pressure[:, 1:], zero_col], 1) - pressure
        grad_depth = jnp.concatenate([pressure[:, :, 1:], zero_dep], 2) - pressure
        vel_inline = vel_inline - COURANT * buoyancy * grad_inline
        vel_xline = vel_xline - COURANT * buoyancy * grad_xline
        vel_depth = vel_depth - COURANT * buoyancy * grad_depth
        divergence = (vel_inline - jnp.concatenate([zero_row, vel_inline[:-1]], 0)) \
            + (vel_xline - jnp.concatenate([zero_col, vel_xline[:, :-1]], 1)) \
            + (vel_depth - jnp.concatenate([zero_dep, vel_depth[:, :, :-1]], 2))
        pressure = pressure - COURANT * modulus * divergence
        pressure = pressure.reshape(-1).at[targets].add(weights * sources[:, step_index]).reshape(field_shape)
    return pressure, vel_inline, vel_xline, vel_depth
```

```python
import functools

import jax
import jax.numpy as jnp
from jax import lax
from jax.experimental import pallas as pl
from jax.experimental.pallas import tpu as pltpu
from jax.sharding import PartitionSpec as P

STEPS = 4
COURANT = 0.35
HALO = 4
REACH = 3
SLOTS = 128
BATCH = 16
PARTS = SLOTS // BATCH
PART_BITS = PARTS.bit_length() - 1
UNROLL = 4
GROUPS = 4
F32 = jnp.float32
BF16 = jnp.bfloat16
ANY = pl.BlockSpec(memory_space=pl.ANY)
VMEM = pl.BlockSpec(memory_space=pltpu.VMEM)
SMEM = pl.BlockSpec(memory_space=pltpu.SMEM)


def rotate(value, axis, steps):
    count = lax.axis_size(axis)
    return lax.ppermute(value, axis, [(source, (source + steps) % count) for source in range(count)])


def iota(shape, dim):
    return lax.broadcasted_iota(jnp.int32, shape, dim)


def lane_before(value):
    lanes = value.ndim - 1
    return jnp.where(iota(value.shape, lanes) == 0, 0.0, pltpu.roll(value, 1, lanes))


def lane_after(value):
    lanes = value.ndim - 1
    width = value.shape[lanes]
    return jnp.where(iota(value.shape, lanes) == width - 1, 0.0, pltpu.roll(value, width - 1, lanes))


def row_before(value):
    return jnp.where(iota(value.shape, 0) == 0, 0.0, pltpu.roll(value, 1, 0))


def half_turn(tile):
    return pltpu.roll(tile, 4, 0)


def run_copies(copies):
    for copy in copies:
        copy.start()
    return copies


def column_pack_kernel(p, vi, vx, vd, m, b, low_out, high_out, strips, sems):
    planes, columns, _ = p.shape
    copies = []
    for side, start in ((0, 0), (1, columns - 8)):
        for field, ref in enumerate((p, vi, vx, vd, m, b)):
            copies.append(
                pltpu.make_async_copy(
                    ref.at[:, pl.ds(start, 8), :], strips.at[side, field], sems.at[side, field]
                )
            )
    run_copies(copies)
    for copy in copies:
        copy.wait()
    upper = iota((8, p.shape[2]), 0) >= 4

    def plane(index, _):
        before = jnp.maximum(index - 1, 0)
        keep = jnp.where(index > 0, 1.0, 0.0)
        for side in range(2):
            sp, svi, svx, svd, sm, sb = (strips.at[side, field] for field in range(6))
            div = (
                (svi[index] - keep * svi[before])
                + (svx[index] - row_before(svx[index]))
                + (svd[index] - lane_before(svd[index]))
            )
            turned_div = half_turn(div)
            turned_b = half_turn(sb[index])
            if side == 0:
                low_out[index, 0:8, :] = jnp.where(upper, turned_div, sp[index])
                low_out[index, 8:16, :] = jnp.where(upper, turned_b, sm[index])
            else:
                first = iota(div.shape, 0) == 0
                edge = jnp.where(first, pltpu.roll(svx[index], 1, 0), turned_div)
                high_out[index, 0:8, :] = jnp.where(upper, sp[index], edge)
                high_out[index, 8:16, :] = jnp.where(upper, sm[index], turned_b)
        return 0

    lax.fori_loop(0, planes, plane, 0, unroll=2)


def column_pack(p, vi, vx, vd, m, b):
    planes, _, depth = p.shape
    out = jax.ShapeDtypeStruct((planes, 16, depth), F32)
    return pl.pallas_call(
        column_pack_kernel,
        out_shape=(out, out),
        in_specs=[ANY] * 6,
        out_specs=(VMEM, VMEM),
        scratch_shapes=[
            pltpu.VMEM((2, 6, planes, 8, depth), F32),
            pltpu.SemaphoreType.DMA((2, 6)),
        ],
        compiler_params=pltpu.CompilerParams(vmem_limit_bytes=60 * 1024 * 1024),
    )(p, vi, vx, vd, m, b)


def plane_pack_kernel(p, vi, vx, vd, m, b, down, up, vel, sems):
    planes, columns, _ = p.shape
    jobs = (
        (vi, 0, 3, vel.at[0, pl.ds(1, 3)]),
        (vx, 0, 3, vel.at[1, pl.ds(1, 3)]),
        (vd, 0, 3, vel.at[2, pl.ds(1, 3)]),
        (vi, planes - 4, 4, vel.at[3]),
        (vx, planes - 4, 4, vel.at[4]),
        (vd, planes - 4, 4, vel.at[5]),
        (p, 0, 4, down.at[pl.ds(0, 4)]),
        (m, 0, 3, down.at[pl.ds(7, 3)]),
        (b, 0, 3, down.at[pl.ds(10, 3)]),
        (p, planes - 4, 4, up.at[pl.ds(0, 4)]),
        (m, planes - 3, 3, up.at[pl.ds(7, 3)]),
        (b, planes - 4, 4, up.at[pl.ds(10, 4)]),
        (vi, planes - 1, 1, up.at[pl.ds(14, 1)]),
    )
    copies = run_copies(
        [
            pltpu.make_async_copy(ref.at[pl.ds(start, count)], target, sems.at[index])
            for index, (ref, start, count, target) in enumerate(jobs)
        ]
    )
    for copy in copies[:6]:
        copy.wait()
    last = columns - 1
    for base, out, line in ((0, down, 13), (3, up, 15)):
        for step in range(1, 4):
            div_i = vel[base, step]
            if base or step > 1:
                div_i = div_i - vel[base, step - 1]
            vx_now = vel[base + 1, step]
            vd_now = vel[base + 2, step]
            out[3 + step] = div_i + (vx_now - row_before(vx_now)) + (vd_now - lane_before(vd_now))
            out[line, step - 1 : step, :] = vel[base + 1, step, last : last + 1, :]
    for copy in copies[6:]:
        copy.wait()


def plane_pack(p, vi, vx, vd, m, b):
    _, columns, depth = p.shape
    return pl.pallas_call(
        plane_pack_kernel,
        out_shape=(
            jax.ShapeDtypeStruct((14, columns, depth), F32),
            jax.ShapeDtypeStruct((16, columns, depth), F32),
        ),
        in_specs=[ANY] * 6,
        out_specs=(VMEM, VMEM),
        scratch_shapes=[pltpu.VMEM((6, 4, columns, depth), F32), pltpu.SemaphoreType.DMA((13,))],
        compiler_params=pltpu.CompilerParams(vmem_limit_bytes=60 * 1024 * 1024),
    )(p, vi, vx, vd, m, b)


def corner_pack_kernel(down, up, low_cols, high_cols, vi, low_out, high_out, dn, upv, row0, vi_last, sems):
    columns = down.shape[1]
    planes = vi.shape[0]
    copies = []
    for side, start in ((0, 0), (1, columns - 8)):
        window = pl.ds(start, 8)
        copies += [
            pltpu.make_async_copy(down.at[pl.ds(0, 13), window, :], dn.at[side], sems.at[side, 0]),
            pltpu.make_async_copy(up.at[pl.ds(0, 15), window, :], upv.at[side], sems.at[side, 1]),
            pltpu.make_async_copy(vi.at[planes - 1, window, :], vi_last.at[side], sems.at[side, 2]),
            pltpu.make_async_copy(
                (low_cols, high_cols)[side].at[0, pl.ds(0, 8), :], row0.at[side], sems.at[side, 3]
            ),
        ]
    lines = [
        pltpu.make_async_copy(up.at[15, pl.ds(0, 8), :], dn.at[2, 0], sems.at[2, 0]),
        pltpu.make_async_copy(down.at[13, pl.ds(0, 8), :], dn.at[2, 1], sems.at[2, 1]),
    ]
    run_copies(copies + lines)
    for copy in copies + lines:
        copy.wait()
    upper = iota((8, down.shape[2]), 0) >= 4
    first = iota((8, down.shape[2]), 0) == 0
    has_before = jnp.where(lax.axis_index("inline") > 0, 1.0, 0.0)
    for side, out in ((0, low_out), (1, high_out)):
        for place in range(9):
            if place == 4:
                fix = half_turn(has_before * upv[side, 14])
                if side == 0:
                    out[place, 0:8, :] = row0[side] - jnp.where(upper, fix, 0.0)
                else:
                    out[place, 0:8, :] = row0[side] - jnp.where(upper | first, 0.0, fix)
                out[place, 8:16, :] = row0[side]
                continue
            if place < 4:
                src = upv.at[side]
                inner = max(place - 1, 0)
                vp, vdiv, vm, vb = src[place], src[4 + inner], src[7 + inner], src[10 + place]
                line = dn[2, 0, inner : inner + 1, :]
            else:
                src = dn.at[side]
                inner = min(place - 5, 2)
                vp, vdiv, vm, vb = src[place - 5], src[4 + inner], src[7 + inner], src[10 + inner]
                line = dn[2, 1, inner : inner + 1, :]
                if place == 5:
                    vdiv = vdiv - vi_last[side]
            if side == 0:
                out[place, 0:8, :] = jnp.where(upper, half_turn(vdiv), vp)
                out[place, 8:16, :] = jnp.where(upper, half_turn(vb), vm)
            else:
                edge = jnp.where(first, line, half_turn(vdiv))
                out[place, 0:8, :] = jnp.where(upper, vp, edge)
                out[place, 8:16, :] = jnp.where(upper, vm, half_turn(vb))


def corner_pack(down, up, low_cols, high_cols, vi):
    depth = down.shape[2]
    out = jax.ShapeDtypeStruct((9, 16, depth), F32)
    return pl.pallas_call(
        corner_pack_kernel,
        out_shape=(out, out),
        in_specs=[ANY] * 5,
        out_specs=(VMEM, VMEM),
        scratch_shapes=[
            pltpu.VMEM((3, 13, 8, depth), F32),
            pltpu.VMEM((2, 15, 8, depth), F32),
            pltpu.VMEM((2, 8, depth), F32),
            pltpu.VMEM((2, 8, depth), F32),
            pltpu.SemaphoreType.DMA((3, 4)),
        ],
        compiler_params=pltpu.CompilerParams(vmem_limit_bytes=60 * 1024 * 1024),
    )(down, up, low_cols, high_cols, vi)


def split3(value):
    high = value.astype(BF16)
    rest = value - high.astype(F32)
    mid = rest.astype(BF16)
    low = (rest - mid.astype(F32)).astype(BF16)
    return high, mid, low


def route_kernel(rounds, n_inline, n_xline, block, traces, resample, owner, cell, out, places):
    planes, columns, depth = block
    nodes = traces.shape[0]
    devices = n_inline * n_xline
    sources = lax.dot_general(
        resample[...],
        traces[...],
        (((1,), (1,)), ((), ())),
        precision=lax.Precision.HIGHEST,
        preferred_element_type=F32,
    )
    own, at = owner[...], cell[...]
    own_x, own_i = own // n_inline, own % n_inline
    at_i, at_j = at // (columns * depth), (at // depth) % columns
    target = iota((devices, 1), 0)
    rel_i = (own_i - target % n_inline) * planes + at_i
    rel_j = (own_x - target // n_inline) * columns + at_j
    off_i = jnp.maximum(jnp.maximum(-rel_i, rel_i - (planes - 1)), 0)
    off_j = jnp.maximum(jnp.maximum(-rel_j, rel_j - (columns - 1)), 0)
    member = off_i + off_j <= REACH
    member_f = jnp.where(member, 1.0, 0.0)
    earlier = jnp.where(iota((nodes, nodes), 0) < iota((nodes, nodes), 1), 1.0, 0.0).astype(BF16)
    place = jnp.dot(member_f.astype(BF16), earlier, preferred_element_type=F32)
    places[...] = jnp.where(member, place, -1.0)
    most = jnp.max(jnp.sum(member_f, axis=1, keepdims=True))
    flag = jnp.where(most > SLOTS, 1024.0, 0.0)

    high, mid, low = split3(sources)
    digits = jnp.concatenate([at % 256, (at // 256) % 256, at // 65536, own + 1], 0).astype(F32).astype(BF16)
    none = jnp.zeros(digits.shape, F32).astype(BF16)
    data = jnp.concatenate([high, digits, mid, none, low, none], 0)
    slot = iota((SLOTS, nodes), 0).astype(F32)
    raised = jnp.where(iota((8, SLOTS), 0) == 4, flag, 0.0)

    def one(index, _):
        device = index % devices
        first = (index // devices + rounds[0]) * SLOTS
        row = places[pl.ds(device, 1), :] - first.astype(F32)
        chosen = jnp.where(slot == row, 1.0, 0.0).astype(BF16)
        packed = lax.dot_general(
            data, chosen, (((1,), (1,)), ((), ())), preferred_element_type=F32
        )
        out[pl.ds(pl.multiple_of(index * 8, 8), 8), :] = (
            packed[0:8] + packed[8:16] + packed[16:24] + raised
        )
        return 0

    lax.fori_loop(0, len(rounds) * devices, one, 0, unroll=4)


def route(traces, resample, owner, cell, rounds, block):
    n_inline, n_xline = lax.axis_size("inline"), lax.axis_size("xline")
    devices = n_inline * n_xline
    nodes = traces.shape[0]
    return pl.pallas_call(
        functools.partial(route_kernel, rounds, n_inline, n_xline, block),
        out_shape=jax.ShapeDtypeStruct((len(rounds) * devices * 8, SLOTS), F32),
        in_specs=[VMEM] * 4,
        out_specs=VMEM,
        scratch_shapes=[pltpu.VMEM((devices, nodes), F32)],
        compiler_params=pltpu.CompilerParams(vmem_limit_bytes=60 * 1024 * 1024),
    )(traces, resample, owner, cell)


def step_kernel(
    rounds, n_inline, n_xline,
    recv, more, over, p, vi, vx, vd, m, b, down, up, right, left, corner_r, corner_l,
    p_out, vi_out, vx_out, vd_out,
    pb, div, mb, bb, inj, v0, v1, v2, p4, vi_before, lines, strip_r, strip_l, cor_r, cor_l,
    lists, codes_v, later_v, parity, counts_v, codes, late_codes, counts, batches, bk, sems, list_sems, out_sems,
):
    planes, columns, depth = p.shape
    rows = columns + 8
    devices = n_inline * n_xline
    at_i, at_x = lax.axis_index("inline"), lax.axis_index("xline")
    own_p, own_c = pl.ds(4, planes), pl.ds(0, columns)
    lane_tiles = depth // 128
    inj_planes = planes + 2 * REACH
    dummy = lane_tiles * inj_planes * rows // 2

    nothing = devices * PARTS
    arrived = lists.at[pl.ds(0, devices * 8), :]
    lists[pl.ds(devices * 8, 8), :] = jnp.zeros((8, SLOTS), F32)
    first_list = pltpu.make_async_copy(recv, arrived, list_sems.at[0])
    first_list.start()
    jobs = (
        (p, pb.at[0, own_p, own_c, :]),
        (b, bb.at[own_p, own_c, :]),
        (m, mb.at[own_p, own_c, :]),
        (vi, v0),
        (vx, v1),
        (vd, v2),
        (up.at[pl.ds(0, 4)], pb.at[0, pl.ds(0, 4), own_c, :]),
        (up.at[pl.ds(4, 3)], div.at[pl.ds(1, 3), own_c, :]),
        (up.at[pl.ds(7, 3)], mb.at[pl.ds(1, 3), own_c, :]),
        (up.at[pl.ds(10, 4)], bb.at[pl.ds(0, 4), own_c, :]),
        (up.at[14], vi_before),
        (up.at[15, pl.ds(0, 8), :], lines.at[0]),
        (down.at[pl.ds(0, 4)], pb.at[0, pl.ds(planes + 4, 4), own_c, :]),
        (down.at[pl.ds(4, 3)], div.at[pl.ds(planes + 4, 3), own_c, :]),
        (down.at[pl.ds(7, 3)], mb.at[pl.ds(planes + 4, 3), own_c, :]),
        (down.at[pl.ds(10, 3)], bb.at[pl.ds(planes + 4, 3), own_c, :]),
        (down.at[13, pl.ds(0, 8), :], lines.at[1]),
        (right, strip_r),
        (left, strip_l),
        (corner_r, cor_r),
        (corner_l, cor_l),
    )
    copies = run_copies(
        [pltpu.make_async_copy(src, dst, sems.at[index]) for index, (src, dst) in enumerate(jobs)]
    )

    def clear(index, _):
        inj[pl.ds(pl.multiple_of(index * rows * STEPS, 8), rows * STEPS), :] = jnp.zeros(
            (rows * STEPS, 128), F32
        )
        return 0

    lax.fori_loop(0, lane_tiles * inj_planes, clear, 0)
    first_list.wait()
    sub = iota((8, SLOTS), 0)
    lane = iota((8, SLOTS), 1)

    def one_round(turn, _):
        @pl.when(turn > 0)
        def _():
            copy = pltpu.make_async_copy(more.at[jnp.maximum(turn - 1, 0)], arrived, list_sems.at[0])
            copy.start()
            copy.wait()

        digit0 = lists[pl.ds(4, devices, stride=8), :]
        digit0 = digit0 - jnp.where(digit0 >= 1024.0, 1024.0, 0.0)
        digit1 = lists[pl.ds(5, devices, stride=8), :]
        digit2 = lists[pl.ds(6, devices, stride=8), :]
        named = lists[pl.ds(7, devices, stride=8), :]
        cell = (digit0 + 256.0 * digit1 + 65536.0 * digit2).astype(jnp.int32)
        own = jnp.maximum(named.astype(jnp.int32) - 1, 0)
        rel_i = (own % n_inline - at_i) * planes + cell // (columns * depth)
        rel_j = (own // n_inline - at_x) * columns + (cell // depth) % columns
        k = cell % depth
        flat = (rel_i + REACH) * rows + jnp.where(rel_j < 0, rel_j + rows, rel_j)
        tile = (k // 128) * (inj_planes * rows // 2) + flat // 2
        slot = iota(tile.shape, 1)
        code = tile * SLOTS + ((k - slot) & (SLOTS - 1))
        parity[...] = flat % 2
        valid = named > 0.0
        tile = jnp.where(valid, tile, -1)
        clash = jnp.zeros(tile.shape, jnp.int32)
        for back in range(1, BATCH):
            same = (pltpu.roll(tile, back, 1) == tile) & (slot % BATCH >= back)
            clash = jnp.where(same, 1, clash)
        now = valid & (clash == 0)
        later = valid & (clash == 1)
        codes_v[0:devices, :] = jnp.where(now, code, dummy * SLOTS)
        codes_v[devices:, :] = jnp.full((8, SLOTS), dummy * SLOTS, jnp.int32)
        later_v[...] = jnp.where(later, code, -1)
        count = jnp.sum(jnp.where(valid, 1.0, 0.0), axis=1, keepdims=True).astype(jnp.int32)
        put_off = jnp.where(later, 1, 0)
        for ahead in (8, 4, 2, 1):
            put_off = jnp.maximum(put_off, pltpu.roll(put_off, SLOTS - ahead, 1))
        any_off = jnp.max(put_off.astype(F32), axis=1, keepdims=True).astype(jnp.int32)
        counts_v[...] = jnp.where(
            slot % BATCH == 0, put_off, jnp.where(slot == 1, count, any_off)
        )
        to_smem = run_copies(
            [
                pltpu.make_async_copy(codes_v, codes, list_sems.at[1]),
                pltpu.make_async_copy(counts_v, counts, list_sems.at[2]),
                pltpu.make_async_copy(later_v, late_codes, list_sems.at[3]),
            ]
        )
        for copy in to_smem:
            copy.wait()

        def one_list(source, total):
            rows8 = pl.ds(pl.multiple_of(source * 8, 8), 8)
            tile8 = lists[rows8, :]
            odd = jnp.broadcast_to(parity[pl.ds(source, 1), :], (8, SLOTS))
            mine = jnp.where(sub < 4, tile8, half_turn(tile8))
            lists[rows8, :] = jnp.where(sub // 4 == odd, COURANT * mine, 0.0)
            for part in range(PARTS):
                batches[total + part] = source * PARTS + part
            return total + (counts[source, 1] + BATCH - 1) // BATCH

        total = lax.fori_loop(0, devices, one_list, 0, unroll=4)
        for extra in range(GROUPS):
            batches[total + extra] = nothing

        def spread(values, code, slot_at):
            alone = jnp.where(lane == slot_at, values, 0.0)
            return pltpu.roll(alone, code & (SLOTS - 1), 1)

        def prepare(index):
            name = batches[index]
            source, base = name >> PART_BITS, (name & (PARTS - 1)) * BATCH
            values = lists[pl.ds(pl.multiple_of(source * 8, 8), 8), :]
            found = [codes[source, base + unit] for unit in range(BATCH)]
            rows_at = [pl.ds(pl.multiple_of((code >> 7) * 8, 8), 8) for code in found]
            return [spread(values, code, base + unit) for unit, code in enumerate(found)], rows_at

        def batch(index, _):
            ready = [prepare(index * GROUPS + group) for group in range(GROUPS)]
            for adds, rows_at in ready:
                sums = [inj[row, :] + add for row, add in zip(rows_at, adds)]
                for row, value in zip(rows_at, sums):
                    inj[row, :] = value
            return 0

        lax.fori_loop(0, (total + GROUPS - 1) // GROUPS, batch, 0)

        def put_off_list(source, _):
            @pl.when(counts[source, 2] > 0)
            def _():
                values = lists[pl.ds(pl.multiple_of(source * 8, 8), 8), :]

                def part_of(part, _):
                    @pl.when(counts[source, part * BATCH] > 0)
                    def _():
                        def single(unit, _):
                            slot_at = part * BATCH + unit
                            code = late_codes[source, slot_at]

                            @pl.when(code >= 0)
                            def _():
                                row = pl.ds(pl.multiple_of((code >> 7) * 8, 8), 8)
                                inj[row, :] += spread(values, code, slot_at)

                            return 0

                        lax.fori_loop(0, BATCH, single, 0)

                    return 0

                lax.fori_loop(0, PARTS, part_of, 0)

            return 0

        lax.fori_loop(0, devices, put_off_list, 0)
        return 0

    lax.fori_loop(0, 1 + over[0] * rounds, one_round, 0)
    for copy in copies:
        copy.wait()

    low_i, high_i = at_i == 0, at_i == n_inline - 1
    low_x, high_x = at_x == 0, at_x == n_xline - 1
    keep_x = jnp.where(low_x, 0.0, 1.0)
    keep_i = jnp.where(low_i, 0.0, 1.0)
    top = iota((8, depth), 0) == 0
    top_own = iota((columns, depth), 0) == 0
    edge = slice(columns, columns + 8)
    upper = iota((8, depth), 0) >= 4
    vi_before[...] = keep_i * vi_before[...]

    def set_strips(plane, a_l, b_l, a_r, b_r, line):
        pb[0, plane, edge, :] = jnp.where(upper, a_l, a_r)
        mb[plane, edge, :] = jnp.where(upper, b_l, b_r)
        bb[plane, edge, :] = half_turn(jnp.where(upper, b_r, b_l))
        turned = half_turn(jnp.where(upper, a_r, a_l))
        div[plane, edge, :] = COURANT * (turned - jnp.where(top, line, 0.0))

    def own_plane(index, before):
        plane = index + 4
        now_i, now_x, now_d = v0[index], v1[index], v2[index]
        tile_a = strip_l[index, 0:8, :]
        set_strips(
            plane, tile_a, strip_l[index, 8:16, :], strip_r[index, 0:8, :], strip_r[index, 8:16, :],
            v1[index, columns - 1 : columns, :],
        )
        x_before = jnp.where(top_own, keep_x * tile_a[0:1, :], pltpu.roll(now_x, 1, 0))
        div[plane, own_c, :] = COURANT * (
            (now_i - before) + (now_x - x_before) + (now_d - lane_before(now_d))
        )
        return now_i

    lax.fori_loop(0, planes, own_plane, vi_before[...], unroll=UNROLL)
    turned = half_turn(jnp.where(upper, cor_r[4, 0:8, :], cor_l[4, 0:8, :]))
    div[4, edge, :] = COURANT * (turned - jnp.where(top, v1[0, columns - 1 : columns, :], 0.0))
    for place in (0, 1, 2, 3, 5, 6, 7, 8):
        plane = place if place < 4 else planes + place - 1
        line_at = max(place - 1, 0) if place < 4 else min(place - 5, 2)
        line = lines[0 if place < 4 else 1, line_at : line_at + 1, :]
        tile_a = cor_l[place, 0:8, :]
        set_strips(
            plane, tile_a, cor_l[place, 8:16, :], cor_r[place, 0:8, :], cor_r[place, 8:16, :], line
        )
        if place not in (0, 8):
            fix = jnp.where(top_own, keep_x * tile_a[0:1, :], 0.0)
            if place == 5:
                fix = fix + v0[planes - 1]
            div[plane, own_c, :] = COURANT * (div[plane, own_c, :] - fix)

    @pl.when(low_i)
    def _():
        bb[0:4] = jnp.zeros((4, rows, depth), F32)

    @pl.when(high_i)
    def _():
        pb[0, planes + 4 :] = jnp.zeros((4, rows, depth), F32)
        mb[planes + 4 :] = jnp.zeros((4, rows, depth), F32)

    @pl.when(low_x)
    def _():
        bb[:, columns + 4 :, :] = jnp.zeros((planes + 8, 4, depth), F32)

    @pl.when(high_x)
    def _():
        pb[0, :, columns : columns + 4, :] = jnp.zeros((planes + 8, 4, depth), F32)
        mb[:, columns : columns + 4, :] = jnp.zeros((planes + 8, 4, depth), F32)

    def shift_buoyancy(plane, _):
        bk[plane] = lane_before(bb[plane])
        return 0

    lax.fori_loop(1, planes + 7, shift_buoyancy, 0, unroll=UNROLL)

    def advance(step, plane, flux_before):
        now, after, buoy = pb[step, plane], pb[step, plane + 1], bb[plane]
        flux_i = buoy * (after - now)
        flux_x = buoy * (pltpu.roll(now, rows - 1, 0) - now)
        change_d = buoy * (lane_after(now) - now) - bk[plane] * (now - pltpu.roll(now, 1, 1))
        change = (
            (flux_i - flux_before)
            + (flux_x - pltpu.roll(flux_x, 1, 0))
            + change_d
        )
        new_div = div[plane] - (COURANT * COURANT) * change
        source = jnp.concatenate(
            [
                inj[pl.ds((part * inj_planes + plane - 1) * rows * STEPS + step, rows, stride=STEPS), :]
                for part in range(lane_tiles)
            ],
            1,
        )
        return flux_i, new_div, now - mb[plane] * (new_div - source)

    for step in range(STEPS - 1):
        def one_plane(plane, flux_before, step=step):
            flux_i, new_div, new_p = advance(step, plane, flux_before)
            div[plane] = new_div
            pb[step + 1, plane] = new_p
            return flux_i

        start = 1 + step
        flux = bb[step] * (pb[step, start] - pb[step, step])
        lax.fori_loop(start, planes + 7 - step, one_plane, flux, unroll=UNROLL)

    last = STEPS - 1

    def total(plane):
        return (pb[0, plane] + pb[1, plane]) + (pb[2, plane] + pb[3, plane])

    def last_plane(index, flux_before):
        plane = index + 4
        flux_i, _, new_p = advance(last, plane, flux_before)
        p4[index] = new_p[:columns]
        here, there = total(plane), total(plane + 1)
        scaled = COURANT * bb[plane, own_c, :]
        mine = here[:columns]
        v0[index] = v0[index] - scaled * (there[:columns] - mine)
        v1[index] = v1[index] - scaled * (pltpu.roll(here, rows - 1, 0)[:columns] - mine)
        v2[index] = v2[index] - scaled * (lane_after(mine) - mine)
        return flux_i

    flux = bb[3] * (pb[last, 4] - pb[last, 3])
    chunk = planes // 8
    outs = []
    for part in range(8):
        flux = lax.fori_loop(part * chunk, (part + 1) * chunk, last_plane, flux, unroll=UNROLL)
        window = pl.ds(part * chunk, chunk)
        outs += run_copies(
            [
                pltpu.make_async_copy(src.at[window], dst.at[window], out_sems.at[part, index])
                for index, (src, dst) in enumerate(
                    ((p4, p_out), (v0, vi_out), (v1, vx_out), (v2, vd_out))
                )
            ]
        )
    for copy in outs:
        copy.wait()


def step_all(recv, more, over, fields, halos):
    p = fields[0]
    planes, columns, depth = p.shape
    n_inline, n_xline = lax.axis_size("inline"), lax.axis_size("xline")
    devices = n_inline * n_xline
    rows = columns + 8
    full = (planes + 8, rows, depth)
    block = (planes, columns, depth)
    inj_rows = (depth // 128) * (planes + 2 * REACH) * rows * STEPS
    return pl.pallas_call(
        functools.partial(step_kernel, more.shape[0], n_inline, n_xline),
        out_shape=tuple(jax.ShapeDtypeStruct(block, F32) for _ in range(4)),
        in_specs=[ANY, ANY, SMEM] + [ANY] * 12,
        out_specs=(ANY,) * 4,
        scratch_shapes=[
            pltpu.VMEM((STEPS,) + full, F32),
            pltpu.VMEM(full, F32),
            pltpu.VMEM(full, F32),
            pltpu.VMEM(full, F32),
            pltpu.VMEM((inj_rows + 8, 128), F32),
            pltpu.VMEM(block, F32),
            pltpu.VMEM(block, F32),
            pltpu.VMEM(block, F32),
            pltpu.VMEM(block, F32),
            pltpu.VMEM((columns, depth), F32),
            pltpu.VMEM((2, 8, depth), F32),
            pltpu.VMEM((planes, 16, depth), F32),
            pltpu.VMEM((planes, 16, depth), F32),
            pltpu.VMEM((9, 16, depth), F32),
            pltpu.VMEM((9, 16, depth), F32),
            pltpu.VMEM((devices * 8 + 8, SLOTS), F32),
            pltpu.VMEM((devices + 8, SLOTS), jnp.int32),
            pltpu.VMEM((devices, SLOTS), jnp.int32),
            pltpu.VMEM((devices, SLOTS), jnp.int32),
            pltpu.VMEM((devices, SLOTS), jnp.int32),
            pltpu.SMEM((devices + 8, SLOTS), jnp.int32),
            pltpu.SMEM((devices, SLOTS), jnp.int32),
            pltpu.SMEM((devices, SLOTS), jnp.int32),
            pltpu.SMEM((devices * PARTS + 2 * GROUPS,), jnp.int32),
            pltpu.VMEM(full, F32),
            pltpu.SemaphoreType.DMA((21,)),
            pltpu.SemaphoreType.DMA((4,)),
            pltpu.SemaphoreType.DMA((8, 4)),
        ],
        compiler_params=pltpu.CompilerParams(vmem_limit_bytes=60 * 1024 * 1024),
    )(recv, more, over, *fields, *halos)


def shards(pressure, vel_inline, vel_xline, vel_depth, modulus, buoyancy, traces, owner, node_cell, resample):
    fields = (pressure, vel_inline, vel_xline, vel_depth, modulus, buoyancy)
    block = pressure.shape
    devices = lax.axis_size("xline") * lax.axis_size("inline")
    nodes = traces.shape[0]
    capacity = max(4, 5 * nodes // (2 * devices))
    most = min(nodes, 9 * capacity)
    rounds = -(-most // SLOTS)

    down_send, up_send = plane_pack(*fields)
    down = rotate(down_send, "inline", -1)
    up = rotate(up_send, "inline", 1)
    low_cols, high_cols = column_pack(*fields)
    right = rotate(low_cols, "xline", -1)
    left = rotate(high_cols, "xline", 1)

    owner_row, cell_row = owner.reshape(1, nodes), node_cell.reshape(1, nodes)
    send = route(traces, resample, owner_row, cell_row, (0,), block)

    def exchange(packed):
        return lax.all_to_all(packed, ("xline", "inline"), split_axis=0, concat_axis=0, tiled=True)

    low_corner, high_corner = corner_pack(down, up, low_cols, high_cols, vel_inline)
    corner_r = rotate(low_corner, "xline", -1)
    corner_l = rotate(high_corner, "xline", 1)
    recv = exchange(send.reshape(devices, 8, SLOTS)).reshape(devices * 8, SLOTS)
    over = jnp.max(recv.reshape(devices, 8, SLOTS)[:, 4, :]) >= 1024.0

    extra = max(1, rounds - 1)

    def spill():
        packed = route(traces, resample, owner_row, cell_row, tuple(range(1, 1 + extra)), block)
        packed = packed.reshape(extra, devices, 8, SLOTS)
        return jnp.stack([exchange(packed[turn]) for turn in range(extra)]).reshape(
            extra, devices * 8, SLOTS
        )

    more = lax.cond(over, spill, lambda: jnp.zeros((extra, devices * 8, SLOTS), F32))
    return step_all(
        recv, more, over.astype(jnp.int32).reshape(1), fields, (down, up, right, left, corner_r, corner_l)
    )


def solution(mesh):
    field = P("inline", "xline", None)
    nodes = ("xline", "inline")
    return jax.shard_map(
        shards,
        mesh=mesh,
        in_specs=(field,) * 6 + (P(nodes, None), P(nodes, None), P(nodes), P()),
        out_specs=(field,) * 4,
        check_vma=False,
    )
```

```python
import functools

import jax
import jax.numpy as jnp
from jax import lax
from jax.experimental import pallas as pl
from jax.experimental.pallas import tpu as pltpu
from jax.sharding import PartitionSpec as P

STEPS = 4
COURANT = 0.35
HALO = 4
REACH = 3
SLOTS = 128
VMEM_LIMIT = 64 * 1024 * 1024
BATCH = 8
PARTS = SLOTS // BATCH
PART_BITS = PARTS.bit_length() - 1
UNROLL = 4
GROUPS = 8
FLAG = 4096.0
F32 = jnp.float32
BF16 = jnp.bfloat16
ANY = pl.BlockSpec(memory_space=pl.ANY)
VMEM = pl.BlockSpec(memory_space=pltpu.VMEM)
SMEM = pl.BlockSpec(memory_space=pltpu.SMEM)


def rotate(value, axis, steps):
    count = lax.axis_size(axis)
    return lax.ppermute(value, axis, [(source, (source + steps) % count) for source in range(count)])


def iota(shape, dim):
    return lax.broadcasted_iota(jnp.int32, shape, dim)


def lane_before(value):
    lanes = value.ndim - 1
    return jnp.where(iota(value.shape, lanes) == 0, 0.0, pltpu.roll(value, 1, lanes))


def lane_after(value):
    lanes = value.ndim - 1
    width = value.shape[lanes]
    return jnp.where(iota(value.shape, lanes) == width - 1, 0.0, pltpu.roll(value, width - 1, lanes))


def row_before(value):
    return jnp.where(iota(value.shape, 0) == 0, 0.0, pltpu.roll(value, 1, 0))


def half_turn(tile):
    return pltpu.roll(tile, 4, 0)


def run_copies(copies):
    for copy in copies:
        copy.start()
    return copies


class Either:
    def __init__(self, choice, first, second, index, target, sem):
        self.choice = choice
        sources = [ref.at[index] if index != () else ref for ref in (first, second)]
        self.copies = [pltpu.make_async_copy(ref, target, sem) for ref in sources]

    def start(self):
        pl.when(self.choice)(self.copies[0].start)
        pl.when(jnp.logical_not(self.choice))(self.copies[1].start)

    def wait(self):
        self.copies[0].wait()


def edge_pack_kernel(
    p, vi, vx, vd, m, b, low_out, high_out, near_out, far_out,
    strips, low, high, down, up, vel, col_sems, sems, out_sems,
):
    planes, columns, depth = p.shape
    col_copies = []
    for side, start in ((0, 0), (1, columns - 8)):
        for field, ref in enumerate((vi, vx, vd, p, m, b)):
            col_copies.append(
                pltpu.make_async_copy(
                    ref.at[:, pl.ds(start, 8), :], strips.at[side, field], col_sems.at[side, field]
                )
            )
    jobs = (
        (vi, 0, 3, vel.at[0, pl.ds(1, 3)]),
        (vx, 0, 3, vel.at[1, pl.ds(1, 3)]),
        (vd, 0, 3, vel.at[2, pl.ds(1, 3)]),
        (vi, planes - 4, 4, vel.at[3]),
        (vx, planes - 4, 4, vel.at[4]),
        (vd, planes - 4, 4, vel.at[5]),
        (p, 0, 4, down.at[pl.ds(0, 4)]),
        (m, 0, 3, down.at[pl.ds(7, 3)]),
        (b, 0, 3, down.at[pl.ds(10, 3)]),
        (p, planes - 4, 4, up.at[pl.ds(0, 4)]),
        (m, planes - 3, 3, up.at[pl.ds(7, 3)]),
        (b, planes - 4, 4, up.at[pl.ds(10, 4)]),
        (vi, planes - 1, 1, up.at[pl.ds(14, 1)]),
    )
    copies = [
        pltpu.make_async_copy(ref.at[pl.ds(start, count)], target, sems.at[index])
        for index, (ref, start, count, target) in enumerate(jobs)
    ]
    run_copies(col_copies + copies)
    upper = iota((8, depth), 0) >= 4
    first = iota((8, depth), 0) == 0
    down[14:16] = jnp.zeros((2, columns, depth), F32)
    for copy in col_copies:
        copy.wait()

    def plane(index, _):
        before = jnp.maximum(index - 1, 0)
        keep = jnp.where(index > 0, 1.0, 0.0)
        for side in range(2):
            svi, svx, svd, sp, sm, sb = (strips.at[side, field] for field in range(6))
            div = (
                (svi[index] - keep * svi[before])
                + (svx[index] - row_before(svx[index]))
                + (svd[index] - lane_before(svd[index]))
            )
            turned_div = half_turn(div)
            turned_b = half_turn(sb[index])
            if side == 0:
                low[index, 0:8, :] = jnp.where(upper, turned_div, sp[index])
                low[index, 8:16, :] = jnp.where(upper, turned_b, sm[index])
            else:
                edge = jnp.where(first, pltpu.roll(svx[index], 1, 0), turned_div)
                high[index, 0:8, :] = jnp.where(upper, sp[index], edge)
                high[index, 8:16, :] = jnp.where(upper, sm[index], turned_b)
        return 0

    lax.fori_loop(0, planes, plane, 0, unroll=8)
    outs = run_copies(
        [
            pltpu.make_async_copy(low, low_out, out_sems.at[0]),
            pltpu.make_async_copy(high, high_out, out_sems.at[1]),
        ]
    )
    for copy in copies[:6]:
        copy.wait()
    last = columns - 1
    for base, out, line in ((0, down, 13), (3, up, 15)):
        for step in range(1, 4):
            div_i = vel[base, step]
            if base or step > 1:
                div_i = div_i - vel[base, step - 1]
            vx_now = vel[base + 1, step]
            vd_now = vel[base + 2, step]
            out[3 + step] = div_i + (vx_now - row_before(vx_now)) + (vd_now - lane_before(vd_now))
            out[line, step - 1 : step, :] = vel[base + 1, step, last : last + 1, :]
    for copy in copies[6:]:
        copy.wait()
    even = lax.axis_index("inline") % 2 == 0
    outs.append(Either(even, up, down, (), near_out, out_sems.at[2]))
    outs.append(Either(even, down, up, (), far_out, out_sems.at[3]))
    run_copies(outs[2:])
    for copy in outs:
        copy.wait()


def edge_pack(p, vi, vx, vd, m, b):
    planes, columns, depth = p.shape
    cols = (planes, 16, depth)
    sheets = (16, columns, depth)
    return pl.pallas_call(
        edge_pack_kernel,
        out_shape=tuple(jax.ShapeDtypeStruct(shape, F32) for shape in (cols, cols, sheets, sheets)),
        in_specs=[ANY] * 6,
        out_specs=(ANY,) * 4,
        scratch_shapes=[
            pltpu.VMEM((2, 6, planes, 8, depth), F32),
            pltpu.VMEM(cols, F32),
            pltpu.VMEM(cols, F32),
            pltpu.VMEM(sheets, F32),
            pltpu.VMEM(sheets, F32),
            pltpu.VMEM((6, 4, columns, depth), F32),
            pltpu.SemaphoreType.DMA((2, 6)),
            pltpu.SemaphoreType.DMA((13,)),
            pltpu.SemaphoreType.DMA((4,)),
        ],
        compiler_params=pltpu.CompilerParams(vmem_limit_bytes=VMEM_LIMIT),
    )(p, vi, vx, vd, m, b)


def corner_rows(side):
    entries = []
    for z in range(2):
        for di in range(1, HALO):
            entries += [(kind, z, di, dj) for dj in range(1, HALO + 1 - di) for kind in "pb"]
            entries += [(kind, z, di, dj) for dj in range(1, HALO - di) for kind in "dm"]
            if side == 1:
                entries.append(("line", z, di, 0))
    return entries + [("first", 0, 0, dj) for dj in range(1, HALO)]


CORNER_ROWS = 48


def corner_pack_kernel(near, far, low_cols, high_cols, vi, low_out, high_out, dn, upv, row0, vi_last, sems):
    columns, depth = near.shape[1:]
    planes = vi.shape[0]
    copies = []
    even = lax.axis_index("inline") % 2 == 0
    for side, start in ((0, 0), (1, columns - 8)):
        window = pl.ds(start, 8)
        copies += [
            Either(even, near, far, (pl.ds(0, 13), window), dn.at[side], sems.at[side, 0]),
            Either(even, far, near, (pl.ds(0, 15), window), upv.at[side], sems.at[side, 1]),
            pltpu.make_async_copy(vi.at[planes - 1, window, :], vi_last.at[side], sems.at[side, 2]),
            pltpu.make_async_copy(
                (low_cols, high_cols)[side].at[0, pl.ds(0, 8), :], row0.at[side], sems.at[side, 3]
            ),
        ]
    lines = [
        Either(even, far, near, (15, pl.ds(0, 8)), dn.at[2, 0], sems.at[2, 0]),
        Either(even, near, far, (13, pl.ds(0, 8)), dn.at[2, 1], sems.at[2, 1]),
    ]
    run_copies(copies + lines)
    for copy in copies + lines:
        copy.wait()
    has_before = lax.axis_index("inline") > 0
    for side, out in ((0, low_out), (1, high_out)):
        out[40:48, :] = jnp.zeros((8, depth), F32)
        for row, (kind, z, di, dj) in enumerate(corner_rows(side)):
            col = dj - 1 if side == 0 else 8 - dj
            at = slice(col, col + 1)
            if kind == "first":
                place = 3 + dj if side == 0 else 4 - dj
                value = row0[side, place : place + 1, :]
                value = value - jnp.where(has_before, upv[side, 14, at, :], 0.0)
            elif kind == "line":
                line = di - 1 if z else 3 - di
                value = dn[2, z, line : line + 1, :]
            elif z:
                value = dn[side, {"p": 0, "d": 4, "m": 7, "b": 10}[kind] + di - 1, at, :]
                if kind == "d" and di == 1:
                    value = value - vi_last[side, at, :]
            else:
                value = upv[side, {"p": 4, "d": 7, "m": 10, "b": 14}[kind] - di, at, :]
            out[row : row + 1, :] = value


def corner_pack(near, far, low_cols, high_cols, vi):
    depth = near.shape[2]
    out = jax.ShapeDtypeStruct((CORNER_ROWS, depth), F32)
    return pl.pallas_call(
        corner_pack_kernel,
        out_shape=(out, out),
        in_specs=[ANY] * 5,
        out_specs=(VMEM, VMEM),
        scratch_shapes=[
            pltpu.VMEM((3, 13, 8, depth), F32),
            pltpu.VMEM((2, 15, 8, depth), F32),
            pltpu.VMEM((2, 8, depth), F32),
            pltpu.VMEM((2, 8, depth), F32),
            pltpu.SemaphoreType.DMA((3, 4)),
        ],
        compiler_params=pltpu.CompilerParams(vmem_limit_bytes=VMEM_LIMIT),
    )(near, far, low_cols, high_cols, vi)


def split3(value):
    high = value.astype(BF16)
    rest = value - high.astype(F32)
    mid = rest.astype(BF16)
    low = (rest - mid.astype(F32)).astype(BF16)
    return high, mid, low


def route_kernel(rounds, n_inline, n_xline, block, traces, resample, owner, cell, out, places):
    planes, columns, depth = block
    nodes = traces.shape[0]
    devices = n_inline * n_xline
    sources = lax.dot_general(
        resample[...],
        traces[...],
        (((1,), (1,)), ((), ())),
        precision=lax.Precision.HIGHEST,
        preferred_element_type=F32,
    )
    own, at = owner[...], cell[...].reshape(1, nodes)
    own_x, own_i = own // n_inline, own % n_inline
    at_i, at_j = at // (columns * depth), (at // depth) % columns
    target = iota((devices, 1), 0)
    rel_i = (own_i - target % n_inline) * planes + at_i
    rel_j = (own_x - target // n_inline) * columns + at_j
    off_i = jnp.maximum(jnp.maximum(-rel_i, rel_i - (planes - 1)), 0)
    off_j = jnp.maximum(jnp.maximum(-rel_j, rel_j - (columns - 1)), 0)
    member = off_i + off_j <= REACH
    member_f = jnp.where(member, 1.0, 0.0)
    earlier = jnp.where(iota((nodes, nodes), 0) < iota((nodes, nodes), 1), 1.0, 0.0).astype(BF16)
    place = jnp.dot(member_f.astype(BF16), earlier, preferred_element_type=F32)
    places[...] = jnp.where(member, place, -1.0)
    most = jnp.max(jnp.sum(member_f, axis=1, keepdims=True))
    flag = jnp.where(most > SLOTS, FLAG, 0.0)

    high, mid, low = split3(sources)
    digits = jnp.concatenate([at % 256, (at // 256) % 256, at // 65536, own + 1], 0).astype(F32).astype(BF16)
    none = jnp.zeros(digits.shape, F32).astype(BF16)
    data = jnp.concatenate([high, digits, mid, none, low, none], 0)
    slot = iota((SLOTS, nodes), 0).astype(F32)
    raised = jnp.where(iota((8, SLOTS), 0) == 4, flag, 0.0)

    def one(index, _):
        device = index % devices
        first = (index // devices + rounds[0]) * SLOTS
        row = places[pl.ds(device, 1), :] - first.astype(F32)
        chosen = jnp.where(slot == row, 1.0, 0.0).astype(BF16)
        packed = lax.dot_general(
            data, chosen, (((1,), (1,)), ((), ())), preferred_element_type=F32
        )
        out[pl.ds(pl.multiple_of(index * 8, 8), 8), :] = (
            packed[0:8] + packed[8:16] + packed[16:24] + raised
        )
        return 0

    lax.fori_loop(0, len(rounds) * devices, one, 0, unroll=16)


def route(traces, resample, owner, cell, rounds, block):
    n_inline, n_xline = lax.axis_size("inline"), lax.axis_size("xline")
    devices = n_inline * n_xline
    nodes = traces.shape[0]
    return pl.pallas_call(
        functools.partial(route_kernel, rounds, n_inline, n_xline, block),
        out_shape=jax.ShapeDtypeStruct((len(rounds) * devices * 8, SLOTS), F32),
        in_specs=[VMEM] * 4,
        out_specs=VMEM,
        scratch_shapes=[pltpu.VMEM((devices, nodes), F32)],
        compiler_params=pltpu.CompilerParams(vmem_limit_bytes=VMEM_LIMIT),
    )(traces, resample, owner, cell)


def step_kernel(
    rounds, n_inline, n_xline, *refs
):
    if rounds:
        more, *refs = refs
    (recv, p, vi, vx, vd, m, b, near, far, right, left, corner_r, corner_l,
    p_out, vi_out, vx_out, vd_out,
    pb, div, mb, bb, inj, v0, v1, v2, p4, bs, lines, strip_r, strip_l, cor_r, cor_l,
    lists, codes_v, later_v, parity, counts_v, codes, late_codes, counts, batches, bk, sems, list_sems, out_sems) = refs
    planes, columns, depth = p.shape
    rows = columns + 8
    devices = n_inline * n_xline
    at_i, at_x = lax.axis_index("inline"), lax.axis_index("xline")
    own_p, own_c = pl.ds(4, planes), pl.ds(0, columns)
    lane_tiles = depth // 128
    inj_planes = planes + 2 * REACH
    dummy = lane_tiles * inj_planes * rows // 2

    nothing = devices * PARTS
    arrived = lists.at[pl.ds(0, devices * 8), :]
    lists[pl.ds(devices * 8, 8), :] = jnp.zeros((8, SLOTS), F32)
    first_list = pltpu.make_async_copy(recv, arrived, list_sems.at[0])
    first_list.start()
    jobs = (
        (vi, v0.at[pl.ds(1, planes)]),
        (vx, v1),
        (vd, v2),
        (b, bb.at[own_p, own_c, :]),
        (right, strip_r),
        (left, strip_l),
        (p, pb.at[0, own_p, own_c, :]),
        (m, mb.at[own_p, own_c, :]),
        (corner_r, cor_r),
        (corner_l, cor_l),
    )
    up_jobs = (
        (pl.ds(0, 4), pb.at[0, pl.ds(0, 4), own_c, :]),
        (pl.ds(4, 3), div.at[pl.ds(1, 3), own_c, :]),
        (pl.ds(7, 3), mb.at[pl.ds(1, 3), own_c, :]),
        (pl.ds(10, 4), bb.at[pl.ds(0, 4), own_c, :]),
        (14, v0.at[0]),
        ((15, pl.ds(0, 8)), lines.at[0]),
    )
    down_jobs = (
        (pl.ds(0, 4), pb.at[0, pl.ds(planes + 4, 4), own_c, :]),
        (pl.ds(4, 3), div.at[pl.ds(planes + 4, 3), own_c, :]),
        (pl.ds(7, 3), mb.at[pl.ds(planes + 4, 3), own_c, :]),
        (pl.ds(10, 3), bb.at[pl.ds(planes + 4, 3), own_c, :]),
        ((13, pl.ds(0, 8)), lines.at[1]),
    )
    even = at_i % 2 == 0
    copies = [pltpu.make_async_copy(src, dst, sems.at[index]) for index, (src, dst) in enumerate(jobs)]
    ups = [
        Either(even, far, near, index, dst, sems.at[10 + job]) for job, (index, dst) in enumerate(up_jobs)
    ]
    downs = [
        Either(even, near, far, index, dst, sems.at[16 + job]) for job, (index, dst) in enumerate(down_jobs)
    ]
    early = run_copies(copies[:6] + [ups[4]])
    late = copies[6:] + ups[:4] + ups[5:] + downs

    def clear(index, _):
        inj[pl.ds(pl.multiple_of(index * rows * STEPS, 8), rows * STEPS), :] = jnp.zeros(
            (rows * STEPS, 128), F32
        )
        return 0

    lax.fori_loop(0, lane_tiles * inj_planes, clear, 0)
    first_list.wait()
    sub = iota((8, SLOTS), 0)
    lane = iota((8, SLOTS), 1)

    low_i, high_i = at_i == 0, at_i == n_inline - 1
    low_x, high_x = at_x == 0, at_x == n_xline - 1
    keep_x = jnp.where(low_x, 0.0, 1.0)
    end_x = jnp.where(high_x, 0.0, 1.0)
    top = iota((8, depth), 0) == 0
    top_own = iota((columns, depth), 0) == 0
    edge = slice(columns, columns + 8)
    upper = iota((8, depth), 0) >= 4
    square = COURANT * COURANT

    def own_plane(index):
        plane = index + 4
        a_l, b_l = strip_l[index, 0:8, :], strip_l[index, 8:16, :]
        a_r, b_r = strip_r[index, 0:8, :], strip_r[index, 8:16, :]
        now_x, now_d = v1[index], v2[index]
        pb[0, plane, edge, :] = jnp.where(upper, a_l, end_x * a_r)
        mb[plane, edge, :] = jnp.where(upper, b_l, end_x * b_r)
        turned = half_turn(jnp.where(upper, a_r, a_l))
        div[plane, edge, :] = COURANT * (turned - jnp.where(top, now_x[columns - 1 : columns, :], 0.0))
        buoy = square * half_turn(jnp.where(upper, b_r, keep_x * b_l))
        bs[plane, edge, :] = buoy
        bk[plane, edge, :] = lane_before(buoy)
        x_before = jnp.where(top_own, keep_x * a_l[0:1, :], pltpu.roll(now_x, 1, 0))
        div[plane, own_c, :] = COURANT * (
            (v0[index + 1] - v0[index]) + (now_x - x_before) + (now_d - lane_before(now_d))
        )
        buoy = square * bb[plane, own_c, :]
        bs[plane, own_c, :] = buoy
        bk[plane, own_c, :] = lane_before(buoy)

    def start_block():
        for copy in early:
            copy.wait()
        run_copies(late)

        @pl.when(low_i)
        def _():
            v0[0] = jnp.zeros((columns, depth), F32)

    def one_round(turn, _):
        if rounds:
            @pl.when(turn > 0)
            def _():
                copy = pltpu.make_async_copy(more.at[jnp.maximum(turn - 1, 0)], arrived, list_sems.at[0])
                copy.start()
                copy.wait()

        digit0 = lists[pl.ds(4, devices, stride=8), :]
        digit0 = digit0 - jnp.where(digit0 >= FLAG, FLAG, 0.0)
        digit1 = lists[pl.ds(5, devices, stride=8), :]
        digit2 = lists[pl.ds(6, devices, stride=8), :]
        named = lists[pl.ds(7, devices, stride=8), :]
        cell = (digit0 + 256.0 * digit1 + 65536.0 * digit2).astype(jnp.int32)
        own = jnp.maximum(named.astype(jnp.int32) - 1, 0)
        rel_i = (own % n_inline - at_i) * planes + cell // (columns * depth)
        rel_j = (own // n_inline - at_x) * columns + (cell // depth) % columns
        k = cell % depth
        flat = (rel_i + REACH) * rows + jnp.where(rel_j < 0, rel_j + rows, rel_j)
        tile = (k // 128) * (inj_planes * rows // 2) + flat // 2
        slot = iota(tile.shape, 1)
        code = tile * SLOTS + ((k - slot) & (SLOTS - 1))
        parity[...] = flat % 2
        valid = named > 0.0
        tile = jnp.where(valid, tile, -1)
        clash = jnp.zeros(tile.shape, jnp.int32)
        for back in range(1, BATCH):
            same = (pltpu.roll(tile, back, 1) == tile) & (slot % BATCH >= back)
            clash = jnp.where(same, 1, clash)
        now = valid & (clash == 0)
        later = valid & (clash == 1)
        codes_v[0:devices, :] = jnp.where(now, code, dummy * SLOTS)
        codes_v[devices:, :] = jnp.full((8, SLOTS), dummy * SLOTS, jnp.int32)
        later_v[...] = jnp.where(later, code, dummy * SLOTS)
        count = jnp.sum(jnp.where(valid, 1.0, 0.0), axis=1, keepdims=True).astype(jnp.int32)
        put_off = jnp.where(later, 1, 0)
        for ahead in (4, 2, 1):
            put_off = jnp.maximum(put_off, pltpu.roll(put_off, SLOTS - ahead, 1))
        any_off = jnp.max(put_off.astype(F32), axis=1, keepdims=True).astype(jnp.int32)
        counts_v[...] = jnp.where(
            slot % BATCH == 0, put_off, jnp.where(slot == 1, count, any_off)
        )
        to_smem = run_copies(
            [
                pltpu.make_async_copy(codes_v, codes, list_sems.at[1]),
                pltpu.make_async_copy(counts_v, counts, list_sems.at[2]),
                pltpu.make_async_copy(later_v, late_codes, list_sems.at[3]),
            ]
        )
        for copy in to_smem:
            copy.wait()

        def one_list(source, total):
            rows8 = pl.ds(pl.multiple_of(source * 8, 8), 8)
            tile8 = lists[rows8, :]
            odd = jnp.broadcast_to(parity[pl.ds(source, 1), :], (8, SLOTS))
            mine = jnp.where(sub < 4, tile8, half_turn(tile8))
            lists[rows8, :] = jnp.where(sub // 4 == odd, COURANT * mine, 0.0)
            for part in range(PARTS):
                batches[total + part] = source * PARTS + part
            return total + (counts[source, 1] + BATCH - 1) // BATCH

        total = lax.fori_loop(0, devices, one_list, 0, unroll=4)

        def pad(index, _):
            for extra in range(GROUPS):
                batches[total + index * GROUPS + extra] = nothing
            return 0

        lax.fori_loop(0, jnp.maximum(planes - total // GROUPS, 1), pad, 0)

        def spread(values, code, slot_at):
            alone = jnp.where(lane == slot_at, values, 0.0)
            return pltpu.roll(alone, code & (SLOTS - 1), 1)

        def prepare(index):
            name = batches[index]
            source, base = name >> PART_BITS, (name & (PARTS - 1)) * BATCH
            values = lists[pl.ds(pl.multiple_of(source * 8, 8), 8), :]
            found = [codes[source, base + unit] for unit in range(BATCH)]
            rows_at = [pl.ds(pl.multiple_of((code >> 7) * 8, 8), 8) for code in found]
            return [spread(values, code, base + unit) for unit, code in enumerate(found)], rows_at

        def batch(index, _):
            ready = [prepare(index * GROUPS + group) for group in range(GROUPS)]
            for adds, rows_at in ready:
                sums = [inj[row, :] + add for row, add in zip(rows_at, adds)]
                for row, value in zip(rows_at, sums):
                    inj[row, :] = value
            own_plane(jnp.minimum(index, planes - 1))
            return 0

        if not rounds:
            start_block()
        turns = jnp.maximum((total + GROUPS - 1) // GROUPS, planes)
        lax.fori_loop(0, turns, batch, 0)

        def put_off_list(source, _):
            @pl.when(counts[source, 2] > 0)
            def _():
                values = lists[pl.ds(pl.multiple_of(source * 8, 8), 8), :]

                def part_of(part, _):
                    @pl.when(counts[source, part * BATCH] > 0)
                    def _():
                        for unit in range(BATCH):
                            slot_at = part * BATCH + unit
                            code = late_codes[source, slot_at]
                            row = pl.ds(pl.multiple_of((code >> 7) * 8, 8), 8)
                            inj[row, :] += spread(values, code, slot_at)

                    return 0

                lax.fori_loop(0, PARTS, part_of, 0)

            return 0

        lax.fori_loop(0, devices, put_off_list, 0)
        return 0

    if rounds:
        start_block()
        lax.fori_loop(0, 1 + rounds, one_round, 0)
    else:
        one_round(0, 0)
    for copy in late:
        copy.wait()

    own_line = v1[0, columns - 1 : columns, :]
    for side, box in ((0, cor_r), (1, cor_l)):
        for row, (kind, z, di, dj) in enumerate(corner_rows(side)):
            plane = planes + 3 + di if z else 4 - di
            spot = columns + dj - 1 if side == 0 else rows - dj
            at = slice(spot, spot + 1)
            value = box[row : row + 1, :]
            line = di - 1 if z else 3 - di
            if kind == "p":
                pb[0, plane, at, :] = value
            elif kind == "b":
                bb[plane, at, :] = value
            elif kind == "m":
                mb[plane, at, :] = value
            elif kind == "line":
                fix = jnp.where(top_own, keep_x * value, 0.0)
                if z and di == 1:
                    fix = fix + v0[planes]
                div[plane, own_c, :] = COURANT * (div[plane, own_c, :] - fix)
            else:
                if side == 0 and dj == 1:
                    value = value - (own_line if kind == "first" else lines[z, line : line + 1, :])
                div[plane, at, :] = COURANT * value

    for first in (0, planes + 4):
        @pl.when(low_x)
        def _(first=first):
            bb[first : first + 4, columns + 4 :, :] = jnp.zeros((4, 4, depth), F32)

        @pl.when(high_x)
        def _(first=first):
            pb[0, first : first + 4, columns : columns + 4, :] = jnp.zeros((4, 4, depth), F32)
            mb[first : first + 4, columns : columns + 4, :] = jnp.zeros((4, 4, depth), F32)

    @pl.when(low_i)
    def _():
        bb[0:4] = jnp.zeros((4, rows, depth), F32)

    @pl.when(high_i)
    def _():
        pb[0, planes + 4 :] = jnp.zeros((4, rows, depth), F32)
        mb[planes + 4 :] = jnp.zeros((4, rows, depth), F32)

    for plane in (0, 1, 2, 3, planes + 4, planes + 5, planes + 6):
        buoy = square * bb[plane]
        bs[plane] = buoy
        bk[plane] = lane_before(buoy)

    def advance(step, plane, flux_before):
        now, after, buoy = pb[step, plane], pb[step, plane + 1], bs[plane]
        flux_i = buoy * (after - now)
        flux_x = buoy * (pltpu.roll(now, rows - 1, 0) - now)
        change_d = buoy * (lane_after(now) - now) - bk[plane] * (now - pltpu.roll(now, 1, 1))
        change = (
            (flux_i - flux_before)
            + (flux_x - pltpu.roll(flux_x, 1, 0))
            + change_d
        )
        new_div = div[plane] - change
        source = jnp.concatenate(
            [
                inj[pl.ds((part * inj_planes + plane - 1) * rows * STEPS + step, rows, stride=STEPS), :]
                for part in range(lane_tiles)
            ],
            1,
        )
        return flux_i, new_div, now - mb[plane] * (new_div - source)

    for step in range(STEPS - 1):
        def one_plane(plane, flux_before, step=step):
            flux_i, new_div, new_p = advance(step, plane, flux_before)
            div[plane] = new_div
            pb[step + 1, plane] = new_p
            return flux_i

        start = 1 + step
        flux = bs[step] * (pb[step, start] - pb[step, step])
        lax.fori_loop(start, planes + 7 - step, one_plane, flux, unroll=UNROLL)

    last = STEPS - 1

    def total(plane):
        return (pb[0, plane] + pb[1, plane]) + (pb[2, plane] + pb[3, plane])

    def last_plane(index, flux_before):
        plane = index + 4
        flux_i, _, new_p = advance(last, plane, flux_before)
        p4[index] = new_p[:columns]
        here, there = total(plane), total(plane + 1)
        scaled = (1.0 / COURANT) * bs[plane, own_c, :]
        mine = here[:columns]
        v0[index + 1] = v0[index + 1] - scaled * (there[:columns] - mine)
        v1[index] = v1[index] - scaled * (pltpu.roll(here, rows - 1, 0)[:columns] - mine)
        v2[index] = v2[index] - scaled * (lane_after(mine) - mine)
        return flux_i

    flux = bs[3] * (pb[last, 4] - pb[last, 3])
    chunk = planes // 8
    outs = []
    for part in range(8):
        flux = lax.fori_loop(part * chunk, (part + 1) * chunk, last_plane, flux, unroll=UNROLL)
        window = pl.ds(part * chunk, chunk)
        outs += run_copies(
            [
                pltpu.make_async_copy(src, dst.at[window], out_sems.at[part, index])
                for index, (src, dst) in enumerate(
                    (
                        (p4.at[window], p_out),
                        (v0.at[pl.ds(part * chunk + 1, chunk)], vi_out),
                        (v1.at[window], vx_out),
                        (v2.at[window], vd_out),
                    )
                )
            ]
        )
    for copy in outs:
        copy.wait()


def step_all(recv, more, fields, halos):
    p = fields[0]
    planes, columns, depth = p.shape
    n_inline, n_xline = lax.axis_size("inline"), lax.axis_size("xline")
    devices = n_inline * n_xline
    rows = columns + 8
    full = (planes + 8, rows, depth)
    block = (planes, columns, depth)
    inj_rows = (depth // 128) * (planes + 2 * REACH) * rows * STEPS
    return pl.pallas_call(
        functools.partial(step_kernel, 0 if more is None else more.shape[0], n_inline, n_xline),
        out_shape=tuple(jax.ShapeDtypeStruct(block, F32) for _ in range(4)),
        in_specs=[ANY] * (13 if more is None else 14),
        out_specs=(ANY,) * 4,
        scratch_shapes=[
            pltpu.VMEM((STEPS,) + full, F32),
            pltpu.VMEM(full, F32),
            pltpu.VMEM(full, F32),
            pltpu.VMEM(full, F32),
            pltpu.VMEM((inj_rows + 8, 128), F32),
            pltpu.VMEM((planes + 1, columns, depth), F32),
            pltpu.VMEM(block, F32),
            pltpu.VMEM(block, F32),
            pltpu.VMEM(block, F32),
            pltpu.VMEM(full, F32),
            pltpu.VMEM((2, 8, depth), F32),
            pltpu.VMEM((planes, 16, depth), F32),
            pltpu.VMEM((planes, 16, depth), F32),
            pltpu.VMEM((CORNER_ROWS, depth), F32),
            pltpu.VMEM((CORNER_ROWS, depth), F32),
            pltpu.VMEM((devices * 8 + 8, SLOTS), F32),
            pltpu.VMEM((devices + 8, SLOTS), jnp.int32),
            pltpu.VMEM((devices, SLOTS), jnp.int32),
            pltpu.VMEM((devices, SLOTS), jnp.int32),
            pltpu.VMEM((devices, SLOTS), jnp.int32),
            pltpu.SMEM((devices + 8, SLOTS), jnp.int32),
            pltpu.SMEM((devices, SLOTS), jnp.int32),
            pltpu.SMEM((devices, SLOTS), jnp.int32),
            pltpu.SMEM((devices * PARTS + (planes + 2) * GROUPS,), jnp.int32),
            pltpu.VMEM(full, F32),
            pltpu.SemaphoreType.DMA((21,)),
            pltpu.SemaphoreType.DMA((4,)),
            pltpu.SemaphoreType.DMA((8, 4)),
        ],
        compiler_params=pltpu.CompilerParams(vmem_limit_bytes=VMEM_LIMIT),
    )(*(() if more is None else (more,)), recv, *fields, *halos)


def shards(pressure, vel_inline, vel_xline, vel_depth, modulus, buoyancy, traces, owner, node_cell, resample):
    fields = (pressure, vel_inline, vel_xline, vel_depth, modulus, buoyancy)
    block = pressure.shape
    devices = lax.axis_size("xline") * lax.axis_size("inline")
    nodes = traces.shape[0]
    capacity = max(4, 5 * nodes // (2 * devices))
    most = min(nodes, 9 * capacity)
    rounds = -(-most // SLOTS)

    low_cols, high_cols, near_send, far_send = edge_pack(*fields)
    right = rotate(low_cols, "xline", -1)
    left = rotate(high_cols, "xline", 1)
    count = lax.axis_size("inline")
    near = lax.ppermute(near_send, "inline", [(source, source ^ 1) for source in range(count)])
    far = lax.ppermute(
        far_send,
        "inline",
        [(source, source if source in (0, count - 1) else ((source - 1) ^ 1) + 1) for source in range(count)],
    )

    owner_row, cell_row = owner.reshape(1, nodes), node_cell
    send = route(traces, resample, owner_row, cell_row, (0,), block)

    def exchange(packed):
        return lax.all_to_all(packed, ("xline", "inline"), split_axis=0, concat_axis=0, tiled=True)

    low_corner, high_corner = corner_pack(near, far, low_cols, high_cols, vel_inline)
    corner_r = rotate(low_corner, "xline", -1)
    corner_l = rotate(high_corner, "xline", 1)
    recv = exchange(send.reshape(devices, 8, SLOTS)).reshape(devices * 8, SLOTS)
    over = jnp.max(recv) >= FLAG / 2
    halos = (near, far, right, left, corner_r, corner_l)

    def spill():
        packed = route(traces, resample, owner_row, cell_row, tuple(range(1, rounds)), block)
        packed = packed.reshape(rounds - 1, devices, 8, SLOTS)
        more = jnp.stack([exchange(packed[turn]) for turn in range(rounds - 1)])
        return step_all(recv, more.reshape(rounds - 1, devices * 8, SLOTS), fields, halos)

    def plain():
        return step_all(recv, None, fields, halos)

    return lax.cond(over, spill, plain) if rounds > 1 else plain()


def solution(mesh):
    field = P("inline", "xline", None)
    nodes = ("xline", "inline")
    return jax.shard_map(
        shards,
        mesh=mesh,
        in_specs=(field,) * 6 + (P(nodes, None), P(nodes, None), P(nodes), P()),
        out_specs=(field,) * 4,
        check_vma=False,
    )
```

```python
import functools

import jax
import jax.numpy as jnp
from jax import lax
from jax.experimental import pallas as pl
from jax.experimental.pallas import tpu as pltpu
from jax.sharding import PartitionSpec as P

STEPS = 4
COURANT = 0.35
HALO = 4
REACH = 3
SLOTS = 128
VMEM_LIMIT = 64 * 1024 * 1024
BATCH = 8
PARTS = SLOTS // BATCH
PART_BITS = PARTS.bit_length() - 1
UNROLL = 4
GROUPS = 8
FLAG = 4096.0
F32 = jnp.float32
BF16 = jnp.bfloat16
ANY = pl.BlockSpec(memory_space=pl.ANY)
VMEM = pl.BlockSpec(memory_space=pltpu.VMEM)
SMEM = pl.BlockSpec(memory_space=pltpu.SMEM)


def rotate(value, axis, steps):
    count = lax.axis_size(axis)
    return lax.ppermute(value, axis, [(source, (source + steps) % count) for source in range(count)])


def iota(shape, dim):
    return lax.broadcasted_iota(jnp.int32, shape, dim)


def lane_before(value):
    lanes = value.ndim - 1
    return jnp.where(iota(value.shape, lanes) == 0, 0.0, pltpu.roll(value, 1, lanes))


def lane_after(value):
    lanes = value.ndim - 1
    width = value.shape[lanes]
    return jnp.where(iota(value.shape, lanes) == width - 1, 0.0, pltpu.roll(value, width - 1, lanes))


def row_before(value):
    return jnp.where(iota(value.shape, 0) == 0, 0.0, pltpu.roll(value, 1, 0))


def half_turn(tile):
    return pltpu.roll(tile, 4, 0)


def run_copies(copies):
    for copy in copies:
        copy.start()
    return copies


class Either:
    def __init__(self, choice, first, second, index, target, sem):
        self.choice = choice
        sources = [ref.at[index] if index != () else ref for ref in (first, second)]
        self.copies = [pltpu.make_async_copy(ref, target, sem) for ref in sources]

    def start(self):
        pl.when(self.choice)(self.copies[0].start)
        pl.when(jnp.logical_not(self.choice))(self.copies[1].start)

    def wait(self):
        self.copies[0].wait()


def edge_pack_kernel(
    p, vi, vx, vd, m, b, low_out, high_out, near_out, far_out,
    strips, low, high, down, up, vel, outer, col_sems, sems, out_sems,
):
    planes, columns, depth = p.shape
    col_copies = []
    for side, start in ((0, 0), (1, columns - 8)):
        for field, ref in enumerate((vi, vx, vd, p, m, b)):
            col_copies.append(
                pltpu.make_async_copy(
                    ref.at[:, pl.ds(start, 8), :], strips.at[side, field], col_sems.at[side, field]
                )
            )
    jobs = (
        (vi, 0, 3, vel.at[0, pl.ds(1, 3)]),
        (vx, 0, 3, vel.at[1, pl.ds(1, 3)]),
        (vd, 0, 3, vel.at[2, pl.ds(1, 3)]),
        (vi, planes - 4, 4, vel.at[3]),
        (vx, planes - 4, 4, vel.at[4]),
        (vd, planes - 4, 4, vel.at[5]),
        (p, 0, 3, down.at[pl.ds(0, 3)]),
        (m, 0, 3, down.at[pl.ds(6, 3)]),
        (b, 0, 3, down.at[pl.ds(9, 3)]),
        (p, planes - 3, 3, up.at[pl.ds(0, 3)]),
        (m, planes - 3, 3, up.at[pl.ds(6, 3)]),
        (b, planes - 3, 3, up.at[pl.ds(9, 3)]),
        (vi, planes - 1, 1, up.at[pl.ds(12, 1)]),
        (p, 3, 1, outer.at[pl.ds(0, 1)]),
        (p, planes - 4, 1, outer.at[pl.ds(1, 1)]),
        (b, planes - 4, 1, outer.at[pl.ds(2, 1)]),
    )
    copies = [
        pltpu.make_async_copy(ref.at[pl.ds(start, count)], target, sems.at[index])
        for index, (ref, start, count, target) in enumerate(jobs)
    ]
    run_copies(col_copies + copies)
    sub = iota((8, depth), 0)
    down[13] = jnp.zeros((columns, depth), F32)
    for copy in col_copies:
        copy.wait()

    def pair(number, _):
        base = pl.multiple_of(number * 24, 8)
        shared = [[], []]
        for half in range(2):
            index = number * 2 + half
            before = jnp.maximum(index - 1, 0)
            keep = jnp.where(index > 0, 1.0, 0.0)
            for side in range(2):
                svi, svx, svd, sp, sm, sb = (strips.at[side, field] for field in range(6))
                now_p, now_m, now_b = sp[index], sm[index], sb[index]
                div = (
                    (svi[index] - keep * svi[before])
                    + (svx[index] - row_before(svx[index]))
                    + (svd[index] - lane_before(svd[index]))
                )
                flux = COURANT * now_b * (pltpu.roll(now_p, 7, 0) - now_p)
                if side == 0:
                    div = jnp.where(sub == 2, div - flux, div)
                    tile = jnp.where(
                        sub < 3, now_p, jnp.where(sub < 6, pltpu.roll(div, 3, 0), pltpu.roll(now_m, 6, 0))
                    )
                    low[pl.ds(base + half * 8, 8), :] = tile
                    rest = jnp.where(sub < 1, pltpu.roll(now_m, 6, 0), pltpu.roll(now_b, 1, 0))
                else:
                    div = jnp.where(sub == 5, div + pltpu.roll(flux, 1, 0), div)
                    tile = jnp.where(
                        sub < 3, pltpu.roll(div, 3, 0), jnp.where(sub < 5, pltpu.roll(now_m, 5, 0), now_p)
                    )
                    high[pl.ds(base + half * 8, 8), :] = tile
                    rest = jnp.where(sub < 1, pltpu.roll(now_m, 3, 0), pltpu.roll(now_b, 4, 0))
                    high[pl.ds(planes * 12 + index, 1), :] = svx[index, 7:8, :]
                shared[side].append(rest)
        for out, (even, odd) in zip((low, high), shared):
            out[pl.ds(base + 16, 8), :] = jnp.where(sub < 4, even, half_turn(odd))
        return 0

    lax.fori_loop(0, planes // 2, pair, 0, unroll=4)
    outs = run_copies(
        [
            pltpu.make_async_copy(low, low_out, out_sems.at[0]),
            pltpu.make_async_copy(high, high_out, out_sems.at[1]),
        ]
    )
    for copy in copies[:6]:
        copy.wait()
    last = columns - 1
    for base, out, line in ((0, down, 12), (3, up, 13)):
        for step in range(1, 4):
            div_i = vel[base, step]
            if base or step > 1:
                div_i = div_i - vel[base, step - 1]
            vx_now = vel[base + 1, step]
            vd_now = vel[base + 2, step]
            out[2 + step] = div_i + (vx_now - row_before(vx_now)) + (vd_now - lane_before(vd_now))
            out[line, step - 1 : step, :] = vel[base + 1, step, last : last + 1, :]
    for copy in copies[6:]:
        copy.wait()
    down[5] = down[5] - COURANT * down[11] * (outer[0] - down[2])
    up[3] = up[3] + COURANT * outer[2] * (up[0] - outer[1])
    even = lax.axis_index("inline") % 2 == 0
    outs.append(Either(even, up, down, (), near_out, out_sems.at[2]))
    outs.append(Either(even, down, up, (), far_out, out_sems.at[3]))
    run_copies(outs[2:])
    for copy in outs:
        copy.wait()


def edge_pack(p, vi, vx, vd, m, b):
    planes, columns, depth = p.shape
    low = (planes * 12, depth)
    high = (planes * 13, depth)
    sheets = (14, columns, depth)
    return pl.pallas_call(
        edge_pack_kernel,
        out_shape=tuple(jax.ShapeDtypeStruct(shape, F32) for shape in (low, high, sheets, sheets)),
        in_specs=[ANY] * 6,
        out_specs=(ANY,) * 4,
        scratch_shapes=[
            pltpu.VMEM((2, 6, planes, 8, depth), F32),
            pltpu.VMEM(low, F32),
            pltpu.VMEM(high, F32),
            pltpu.VMEM(sheets, F32),
            pltpu.VMEM(sheets, F32),
            pltpu.VMEM((6, 4, columns, depth), F32),
            pltpu.VMEM((3, columns, depth), F32),
            pltpu.SemaphoreType.DMA((2, 6)),
            pltpu.SemaphoreType.DMA((16,)),
            pltpu.SemaphoreType.DMA((4,)),
        ],
        compiler_params=pltpu.CompilerParams(vmem_limit_bytes=VMEM_LIMIT),
    )(p, vi, vx, vd, m, b)


def corner_rows(side):
    entries = []
    for z in range(2):
        for di in range(1, HALO):
            entries += [(kind, z, di, dj) for dj in range(1, HALO + 1 - di) for kind in "pb"]
            entries += [(kind, z, di, dj) for dj in range(1, HALO - di) for kind in "dm"]
            if side == 1:
                entries.append(("line", z, di, 0))
    return entries + [("first", 0, 0, dj) for dj in range(1, HALO)]


CORNER_ROWS = 48


def corner_pack_kernel(near, far, low_cols, high_cols, vi, low_out, high_out, dn, upv, row0, vi_last, sems):
    columns, depth = near.shape[1:]
    planes = vi.shape[0]
    copies = []
    even = lax.axis_index("inline") % 2 == 0
    for side, start in ((0, 0), (1, columns - 8)):
        window = pl.ds(start, 8)
        copies += [
            Either(even, near, far, (pl.ds(0, 12), window), dn.at[side], sems.at[side, 0]),
            Either(even, far, near, (pl.ds(0, 13), window), upv.at[side], sems.at[side, 1]),
            pltpu.make_async_copy(vi.at[planes - 1, window, :], vi_last.at[side], sems.at[side, 2]),
            pltpu.make_async_copy(
                (low_cols, high_cols)[side].at[pl.ds(0, 8), :], row0.at[side], sems.at[side, 3]
            ),
        ]
    lines = [
        Either(even, far, near, (13, pl.ds(0, 8)), dn.at[2, 0], sems.at[2, 0]),
        Either(even, near, far, (12, pl.ds(0, 8)), dn.at[2, 1], sems.at[2, 1]),
    ]
    run_copies(copies + lines)
    for copy in copies + lines:
        copy.wait()
    has_before = lax.axis_index("inline") > 0
    for side, out in ((0, low_out), (1, high_out)):
        out[40:48, :] = jnp.zeros((8, depth), F32)
        for row, (kind, z, di, dj) in enumerate(corner_rows(side)):
            col = dj - 1 if side == 0 else 8 - dj
            at = slice(col, col + 1)
            if kind == "first":
                place = 2 + dj if side == 0 else 3 - dj
                value = row0[side, place : place + 1, :]
                value = value - jnp.where(has_before, upv[side, 12, at, :], 0.0)
            elif kind == "line":
                line = di - 1 if z else 3 - di
                value = dn[2, z, line : line + 1, :]
            elif z:
                value = dn[side, {"p": 0, "d": 3, "m": 6, "b": 9}[kind] + di - 1, at, :]
                if kind == "d" and di == 1:
                    value = value - vi_last[side, at, :]
            else:
                value = upv[side, {"p": 3, "d": 6, "m": 9, "b": 12}[kind] - di, at, :]
            out[row : row + 1, :] = value


def corner_pack(near, far, low_cols, high_cols, vi):
    depth = near.shape[2]
    out = jax.ShapeDtypeStruct((CORNER_ROWS, depth), F32)
    return pl.pallas_call(
        corner_pack_kernel,
        out_shape=(out, out),
        in_specs=[ANY] * 5,
        out_specs=(VMEM, VMEM),
        scratch_shapes=[
            pltpu.VMEM((3, 12, 8, depth), F32),
            pltpu.VMEM((2, 13, 8, depth), F32),
            pltpu.VMEM((2, 8, depth), F32),
            pltpu.VMEM((2, 8, depth), F32),
            pltpu.SemaphoreType.DMA((3, 4)),
        ],
        compiler_params=pltpu.CompilerParams(vmem_limit_bytes=VMEM_LIMIT),
    )(near, far, low_cols, high_cols, vi)


def split3(value):
    high = value.astype(BF16)
    rest = value - high.astype(F32)
    mid = rest.astype(BF16)
    low = (rest - mid.astype(F32)).astype(BF16)
    return high, mid, low


def route_kernel(rounds, n_inline, n_xline, block, traces, resample, owner, cell, out, places):
    planes, columns, depth = block
    nodes = traces.shape[0]
    devices = n_inline * n_xline
    sources = lax.dot_general(
        resample[...],
        traces[...],
        (((1,), (1,)), ((), ())),
        precision=lax.Precision.HIGHEST,
        preferred_element_type=F32,
    )
    own, at = owner[...], cell[...].reshape(1, nodes)
    own_x, own_i = own // n_inline, own % n_inline
    at_i, at_j = at // (columns * depth), (at // depth) % columns
    target = iota((devices, 1), 0)
    rel_i = (own_i - target % n_inline) * planes + at_i
    rel_j = (own_x - target // n_inline) * columns + at_j
    off_i = jnp.maximum(jnp.maximum(-rel_i, rel_i - (planes - 1)), 0)
    off_j = jnp.maximum(jnp.maximum(-rel_j, rel_j - (columns - 1)), 0)
    member = off_i + off_j <= REACH
    member_f = jnp.where(member, 1.0, 0.0)
    earlier = jnp.where(iota((nodes, nodes), 0) < iota((nodes, nodes), 1), 1.0, 0.0).astype(BF16)
    place = jnp.dot(member_f.astype(BF16), earlier, preferred_element_type=F32)
    places[...] = jnp.where(member, place, -1.0)
    most = jnp.max(jnp.sum(member_f, axis=1, keepdims=True))
    flag = jnp.where(most > SLOTS, FLAG, 0.0)

    high, mid, low = split3(sources)
    digits = jnp.concatenate([at % 256, (at // 256) % 256, at // 65536, own + 1], 0).astype(F32).astype(BF16)
    none = jnp.zeros(digits.shape, F32).astype(BF16)
    data = jnp.concatenate([high, digits, mid, none, low, none], 0)
    slot = iota((SLOTS, nodes), 0).astype(F32)
    raised = jnp.where(iota((8, SLOTS), 0) == 4, flag, 0.0)

    def one(index, _):
        device = index % devices
        first = (index // devices + rounds[0]) * SLOTS
        row = places[pl.ds(device, 1), :] - first.astype(F32)
        chosen = jnp.where(slot == row, 1.0, 0.0).astype(BF16)
        packed = lax.dot_general(
            data, chosen, (((1,), (1,)), ((), ())), preferred_element_type=F32
        )
        out[pl.ds(pl.multiple_of(index * 8, 8), 8), :] = (
            packed[0:8] + packed[8:16] + packed[16:24] + raised
        )
        return 0

    lax.fori_loop(0, len(rounds) * devices, one, 0, unroll=16)


def route(traces, resample, owner, cell, rounds, block):
    n_inline, n_xline = lax.axis_size("inline"), lax.axis_size("xline")
    devices = n_inline * n_xline
    nodes = traces.shape[0]
    return pl.pallas_call(
        functools.partial(route_kernel, rounds, n_inline, n_xline, block),
        out_shape=jax.ShapeDtypeStruct((len(rounds) * devices * 8, SLOTS), F32),
        in_specs=[VMEM] * 4,
        out_specs=VMEM,
        scratch_shapes=[pltpu.VMEM((devices, nodes), F32)],
        compiler_params=pltpu.CompilerParams(vmem_limit_bytes=VMEM_LIMIT),
    )(traces, resample, owner, cell)


def step_kernel(
    rounds, n_inline, n_xline, *refs
):
    if rounds:
        more, *refs = refs
    (recv, p, vi, vx, vd, m, b, near, far, right, left, corner_r, corner_l,
    p_out, vi_out, vx_out, vd_out,
    pb, div, mb, bb, inj, v0, v1, v2, p4, bs, lines, strip_r, strip_l, cor_r, cor_l,
    lists, codes_v, later_v, parity, counts_v, codes, late_codes, counts, batches, bk, sems, list_sems, out_sems) = refs
    planes, columns, depth = p.shape
    rows = columns + 8
    devices = n_inline * n_xline
    at_i, at_x = lax.axis_index("inline"), lax.axis_index("xline")
    own_p, own_c = pl.ds(4, planes), pl.ds(0, columns)
    lane_tiles = depth // 128
    inj_planes = planes + 2 * REACH
    dummy = lane_tiles * inj_planes * rows // 2

    nothing = devices * PARTS
    arrived = lists.at[pl.ds(0, devices * 8), :]
    lists[pl.ds(devices * 8, 8), :] = jnp.zeros((8, SLOTS), F32)
    first_list = pltpu.make_async_copy(recv, arrived, list_sems.at[0])
    first_list.start()
    jobs = (
        (vi, v0.at[pl.ds(1, planes)]),
        (vx, v1),
        (vd, v2),
        (b, bb.at[own_p, own_c, :]),
        (right, strip_r),
        (left, strip_l),
        (p, pb.at[0, own_p, own_c, :]),
        (m, mb.at[own_p, own_c, :]),
        (corner_r, cor_r),
        (corner_l, cor_l),
    )
    up_jobs = (
        (pl.ds(0, 3), pb.at[0, pl.ds(1, 3), own_c, :]),
        (pl.ds(3, 3), div.at[pl.ds(1, 3), own_c, :]),
        (pl.ds(6, 3), mb.at[pl.ds(1, 3), own_c, :]),
        (pl.ds(9, 3), bb.at[pl.ds(1, 3), own_c, :]),
        (12, v0.at[0]),
        ((13, pl.ds(0, 8)), lines.at[0]),
    )
    down_jobs = (
        (pl.ds(0, 3), pb.at[0, pl.ds(planes + 4, 3), own_c, :]),
        (pl.ds(3, 3), div.at[pl.ds(planes + 4, 3), own_c, :]),
        (pl.ds(6, 3), mb.at[pl.ds(planes + 4, 3), own_c, :]),
        (pl.ds(9, 3), bb.at[pl.ds(planes + 4, 3), own_c, :]),
        ((12, pl.ds(0, 8)), lines.at[1]),
    )
    even = at_i % 2 == 0
    copies = [pltpu.make_async_copy(src, dst, sems.at[index]) for index, (src, dst) in enumerate(jobs)]
    ups = [
        Either(even, far, near, index, dst, sems.at[10 + job]) for job, (index, dst) in enumerate(up_jobs)
    ]
    downs = [
        Either(even, near, far, index, dst, sems.at[16 + job]) for job, (index, dst) in enumerate(down_jobs)
    ]
    early = run_copies(copies[:6] + [ups[4]])
    late = copies[6:] + ups[:4] + ups[5:] + downs

    def clear(index, _):
        inj[pl.ds(pl.multiple_of(index * rows * STEPS, 8), rows * STEPS), :] = jnp.zeros(
            (rows * STEPS, 128), F32
        )
        return 0

    lax.fori_loop(0, lane_tiles * inj_planes, clear, 0)
    first_list.wait()
    sub = iota((8, SLOTS), 0)
    lane = iota((8, SLOTS), 1)

    low_i, high_i = at_i == 0, at_i == n_inline - 1
    low_x, high_x = at_x == 0, at_x == n_xline - 1
    keep_x = jnp.where(low_x, 0.0, 1.0)
    end_x = jnp.where(high_x, 0.0, 1.0)
    top = iota((8, depth), 0) == 0
    top_own = iota((columns, depth), 0) == 0
    edge = slice(columns, columns + 8)
    sub_d = iota((8, depth), 0)
    upper = sub_d >= 4
    square = COURANT * COURANT

    def own_plane(index):
        plane = index + 4
        pair, odd = index // 2, index % 2
        tile_at = pl.ds(pl.multiple_of(pair * 24 + odd * 8, 8), 8)
        rest_at = pl.ds(pl.multiple_of(pair * 24 + 16, 8), 8)
        t_l, t_r = strip_l[tile_at, :], strip_r[tile_at, :]
        rest_l, rest_r = strip_l[rest_at, :], strip_r[rest_at, :]
        rest_l = jnp.where(odd == 1, half_turn(rest_l), rest_l)
        rest_r = jnp.where(odd == 1, half_turn(rest_r), rest_r)
        vx_l = keep_x * strip_l[pl.ds(planes * 12 + index, 1), :]
        now_x, now_d = v1[index], v2[index]
        p_l = jnp.where(sub_d == 4, pltpu.roll(t_l, 7, 0), t_l)
        p_r = jnp.where(sub_d == 3, pltpu.roll(t_r, 1, 0), t_r)
        pb[0, plane, edge, :] = jnp.where(upper, p_l, end_x * p_r)
        m_l = jnp.where(sub_d == 5, pltpu.roll(rest_l, 5, 0), pltpu.roll(t_l, 3, 0))
        m_r = jnp.where(sub_d == 2, pltpu.roll(rest_r, 2, 0), pltpu.roll(t_r, 2, 0))
        mb[plane, edge, :] = jnp.where(upper, m_l, end_x * m_r)
        turned = pltpu.roll(jnp.where((sub_d >= 3) & (sub_d < 6), t_r, t_l), 5, 0)
        div[plane, edge, :] = COURANT * (turned - jnp.where(top, now_x[columns - 1 : columns, :], 0.0))
        buoy = square * jnp.where(upper, keep_x * half_turn(rest_l), pltpu.roll(rest_r, 7, 0))
        bs[plane, edge, :] = buoy
        bk[plane, edge, :] = lane_before(buoy)
        x_before = jnp.where(top_own, vx_l, pltpu.roll(now_x, 1, 0))
        div[plane, own_c, :] = COURANT * (
            (v0[index + 1] - v0[index]) + (now_x - x_before) + (now_d - lane_before(now_d))
        )
        buoy = square * bb[plane, own_c, :]
        bs[plane, own_c, :] = buoy
        bk[plane, own_c, :] = lane_before(buoy)

    def start_block():
        for copy in early:
            copy.wait()
        run_copies(late)

        @pl.when(low_i)
        def _():
            v0[0] = jnp.zeros((columns, depth), F32)

    def one_round(turn, _):
        if rounds:
            @pl.when(turn > 0)
            def _():
                copy = pltpu.make_async_copy(more.at[jnp.maximum(turn - 1, 0)], arrived, list_sems.at[0])
                copy.start()
                copy.wait()

        digit0 = lists[pl.ds(4, devices, stride=8), :]
        digit0 = digit0 - jnp.where(digit0 >= FLAG, FLAG, 0.0)
        digit1 = lists[pl.ds(5, devices, stride=8), :]
        digit2 = lists[pl.ds(6, devices, stride=8), :]
        named = lists[pl.ds(7, devices, stride=8), :]
        cell = (digit0 + 256.0 * digit1 + 65536.0 * digit2).astype(jnp.int32)
        own = jnp.maximum(named.astype(jnp.int32) - 1, 0)
        rel_i = (own % n_inline - at_i) * planes + cell // (columns * depth)
        rel_j = (own // n_inline - at_x) * columns + (cell // depth) % columns
        k = cell % depth
        flat = (rel_i + REACH) * rows + jnp.where(rel_j < 0, rel_j + rows, rel_j)
        tile = (k // 128) * (inj_planes * rows // 2) + flat // 2
        slot = iota(tile.shape, 1)
        code = tile * SLOTS + ((k - slot) & (SLOTS - 1))
        parity[...] = flat % 2
        valid = named > 0.0
        tile = jnp.where(valid, tile, -1)
        clash = jnp.zeros(tile.shape, jnp.int32)
        for back in range(1, BATCH):
            same = (pltpu.roll(tile, back, 1) == tile) & (slot % BATCH >= back)
            clash = jnp.where(same, 1, clash)
        now = valid & (clash == 0)
        later = valid & (clash == 1)
        codes_v[0:devices, :] = jnp.where(now, code, dummy * SLOTS)
        codes_v[devices:, :] = jnp.full((8, SLOTS), dummy * SLOTS, jnp.int32)
        later_v[...] = jnp.where(later, code, dummy * SLOTS)
        count = jnp.sum(jnp.where(valid, 1.0, 0.0), axis=1, keepdims=True).astype(jnp.int32)
        put_off = jnp.where(later, 1, 0)
        for ahead in (4, 2, 1):
            put_off = jnp.maximum(put_off, pltpu.roll(put_off, SLOTS - ahead, 1))
        any_off = jnp.max(put_off.astype(F32), axis=1, keepdims=True).astype(jnp.int32)
        counts_v[...] = jnp.where(
            slot % BATCH == 0, put_off, jnp.where(slot == 1, count, any_off)
        )
        to_smem = run_copies(
            [
                pltpu.make_async_copy(codes_v, codes, list_sems.at[1]),
                pltpu.make_async_copy(counts_v, counts, list_sems.at[2]),
                pltpu.make_async_copy(later_v, late_codes, list_sems.at[3]),
            ]
        )
        for copy in to_smem:
            copy.wait()

        def one_list(source, total):
            rows8 = pl.ds(pl.multiple_of(source * 8, 8), 8)
            tile8 = lists[rows8, :]
            odd = jnp.broadcast_to(parity[pl.ds(source, 1), :], (8, SLOTS))
            mine = jnp.where(sub < 4, tile8, half_turn(tile8))
            lists[rows8, :] = jnp.where(sub // 4 == odd, COURANT * mine, 0.0)
            for part in range(PARTS):
                batches[total + part] = source * PARTS + part
            return total + (counts[source, 1] + BATCH - 1) // BATCH

        total = lax.fori_loop(0, devices, one_list, 0, unroll=4)

        def pad(index, _):
            for extra in range(GROUPS):
                batches[total + index * GROUPS + extra] = nothing
            return 0

        lax.fori_loop(0, jnp.maximum(planes - total // GROUPS, 1), pad, 0)

        def spread(values, code, slot_at):
            alone = jnp.where(lane == slot_at, values, 0.0)
            return pltpu.roll(alone, code & (SLOTS - 1), 1)

        def prepare(index):
            name = batches[index]
            source, base = name >> PART_BITS, (name & (PARTS - 1)) * BATCH
            values = lists[pl.ds(pl.multiple_of(source * 8, 8), 8), :]
            found = [codes[source, base + unit] for unit in range(BATCH)]
            rows_at = [pl.ds(pl.multiple_of((code >> 7) * 8, 8), 8) for code in found]
            return [spread(values, code, base + unit) for unit, code in enumerate(found)], rows_at

        def batch(index, _):
            ready = [prepare(index * GROUPS + group) for group in range(GROUPS)]
            for adds, rows_at in ready:
                sums = [inj[row, :] + add for row, add in zip(rows_at, adds)]
                for row, value in zip(rows_at, sums):
                    inj[row, :] = value
            own_plane(jnp.minimum(index, planes - 1))
            return 0

        if not rounds:
            start_block()
        turns = jnp.maximum((total + GROUPS - 1) // GROUPS, planes)
        lax.fori_loop(0, turns, batch, 0)

        def put_off_list(source, _):
            @pl.when(counts[source, 2] > 0)
            def _():
                values = lists[pl.ds(pl.multiple_of(source * 8, 8), 8), :]

                def part_of(part, _):
                    @pl.when(counts[source, part * BATCH] > 0)
                    def _():
                        for unit in range(BATCH):
                            slot_at = part * BATCH + unit
                            code = late_codes[source, slot_at]
                            row = pl.ds(pl.multiple_of((code >> 7) * 8, 8), 8)
                            inj[row, :] += spread(values, code, slot_at)

                    return 0

                lax.fori_loop(0, PARTS, part_of, 0)

            return 0

        lax.fori_loop(0, devices, put_off_list, 0)
        return 0

    if rounds:
        start_block()
        lax.fori_loop(0, 1 + rounds, one_round, 0)
    else:
        one_round(0, 0)
    for copy in late:
        copy.wait()

    bb[0] = jnp.zeros((rows, depth), F32)
    pb[0, 0, own_c, :] = pb[0, 1, own_c, :]
    pb[0, planes + 7, own_c, :] = pb[0, planes + 6, own_c, :]
    own_line = v1[0, columns - 1 : columns, :]
    for side, box in ((0, cor_r), (1, cor_l)):
        for row, (kind, z, di, dj) in enumerate(corner_rows(side)):
            plane = planes + 3 + di if z else 4 - di
            spot = columns + dj - 1 if side == 0 else rows - dj
            at = slice(spot, spot + 1)
            value = box[row : row + 1, :]
            line = di - 1 if z else 3 - di
            if kind == "p":
                pb[0, plane, at, :] = value
            elif kind == "b":
                bb[plane, at, :] = value
            elif kind == "m":
                mb[plane, at, :] = value
            elif kind == "line":
                fix = jnp.where(top_own, keep_x * value, 0.0)
                if z and di == 1:
                    fix = fix + v0[planes]
                div[plane, own_c, :] = COURANT * (div[plane, own_c, :] - fix)
            else:
                if side == 0 and dj == 1:
                    value = value - (own_line if kind == "first" else lines[z, line : line + 1, :])
                div[plane, at, :] = COURANT * value

    for first in (0, planes + 4):
        @pl.when(low_x)
        def _(first=first):
            bb[first : first + 4, columns + 4 :, :] = jnp.zeros((4, 4, depth), F32)

        @pl.when(high_x)
        def _(first=first):
            pb[0, first : first + 4, columns : columns + 4, :] = jnp.zeros((4, 4, depth), F32)
            mb[first : first + 4, columns : columns + 4, :] = jnp.zeros((4, 4, depth), F32)

    @pl.when(low_i)
    def _():
        bb[0:4] = jnp.zeros((4, rows, depth), F32)

    @pl.when(high_i)
    def _():
        pb[0, planes + 4 :] = jnp.zeros((4, rows, depth), F32)
        mb[planes + 4 :] = jnp.zeros((4, rows, depth), F32)

    for plane in (0, 1, 2, 3, planes + 4, planes + 5, planes + 6):
        buoy = square * bb[plane]
        bs[plane] = buoy
        bk[plane] = lane_before(buoy)

    def advance(step, plane, flux_before):
        now, after, buoy = pb[step, plane], pb[step, plane + 1], bs[plane]
        flux_i = buoy * (after - now)
        flux_x = buoy * (pltpu.roll(now, rows - 1, 0) - now)
        change_d = buoy * (lane_after(now) - now) - bk[plane] * (now - pltpu.roll(now, 1, 1))
        change = (
            (flux_i - flux_before)
            + (flux_x - pltpu.roll(flux_x, 1, 0))
            + change_d
        )
        new_div = div[plane] - change
        source = jnp.concatenate(
            [
                inj[pl.ds((part * inj_planes + plane - 1) * rows * STEPS + step, rows, stride=STEPS), :]
                for part in range(lane_tiles)
            ],
            1,
        )
        return flux_i, new_div, now - mb[plane] * (new_div - source)

    for step in range(STEPS - 1):
        def one_plane(plane, flux_before, step=step):
            flux_i, new_div, new_p = advance(step, plane, flux_before)
            div[plane] = new_div
            pb[step + 1, plane] = new_p
            return flux_i

        start = 1 + step
        flux = bs[step] * (pb[step, start] - pb[step, step])
        lax.fori_loop(start, planes + 7 - step, one_plane, flux, unroll=UNROLL)

    last = STEPS - 1

    def total(plane):
        return (pb[0, plane] + pb[1, plane]) + (pb[2, plane] + pb[3, plane])

    def last_plane(index, flux_before):
        plane = index + 4
        flux_i, _, new_p = advance(last, plane, flux_before)
        p4[index] = new_p[:columns]
        here, there = total(plane), total(plane + 1)
        scaled = (1.0 / COURANT) * bs[plane, own_c, :]
        mine = here[:columns]
        v0[index + 1] = v0[index + 1] - scaled * (there[:columns] - mine)
        v1[index] = v1[index] - scaled * (pltpu.roll(here, rows - 1, 0)[:columns] - mine)
        v2[index] = v2[index] - scaled * (lane_after(mine) - mine)
        return flux_i

    flux = bs[3] * (pb[last, 4] - pb[last, 3])
    chunk = planes // 8
    outs = []
    for part in range(8):
        flux = lax.fori_loop(part * chunk, (part + 1) * chunk, last_plane, flux, unroll=UNROLL)
        window = pl.ds(part * chunk, chunk)
        outs += run_copies(
            [
                pltpu.make_async_copy(src, dst.at[window], out_sems.at[part, index])
                for index, (src, dst) in enumerate(
                    (
                        (p4.at[window], p_out),
                        (v0.at[pl.ds(part * chunk + 1, chunk)], vi_out),
                        (v1.at[window], vx_out),
                        (v2.at[window], vd_out),
                    )
                )
            ]
        )
    for copy in outs:
        copy.wait()


def step_all(recv, more, fields, halos):
    p = fields[0]
    planes, columns, depth = p.shape
    n_inline, n_xline = lax.axis_size("inline"), lax.axis_size("xline")
    devices = n_inline * n_xline
    rows = columns + 8
    full = (planes + 8, rows, depth)
    block = (planes, columns, depth)
    inj_rows = (depth // 128) * (planes + 2 * REACH) * rows * STEPS
    return pl.pallas_call(
        functools.partial(step_kernel, 0 if more is None else more.shape[0], n_inline, n_xline),
        out_shape=tuple(jax.ShapeDtypeStruct(block, F32) for _ in range(4)),
        in_specs=[ANY] * (13 if more is None else 14),
        out_specs=(ANY,) * 4,
        scratch_shapes=[
            pltpu.VMEM((STEPS,) + full, F32),
            pltpu.VMEM(full, F32),
            pltpu.VMEM(full, F32),
            pltpu.VMEM(full, F32),
            pltpu.VMEM((inj_rows + 8, 128), F32),
            pltpu.VMEM((planes + 1, columns, depth), F32),
            pltpu.VMEM(block, F32),
            pltpu.VMEM(block, F32),
            pltpu.VMEM(block, F32),
            pltpu.VMEM(full, F32),
            pltpu.VMEM((2, 8, depth), F32),
            pltpu.VMEM((planes * 12, depth), F32),
            pltpu.VMEM((planes * 13, depth), F32),
            pltpu.VMEM((CORNER_ROWS, depth), F32),
            pltpu.VMEM((CORNER_ROWS, depth), F32),
            pltpu.VMEM((devices * 8 + 8, SLOTS), F32),
            pltpu.VMEM((devices + 8, SLOTS), jnp.int32),
            pltpu.VMEM((devices, SLOTS), jnp.int32),
            pltpu.VMEM((devices, SLOTS), jnp.int32),
            pltpu.VMEM((devices, SLOTS), jnp.int32),
            pltpu.SMEM((devices + 8, SLOTS), jnp.int32),
            pltpu.SMEM((devices, SLOTS), jnp.int32),
            pltpu.SMEM((devices, SLOTS), jnp.int32),
            pltpu.SMEM((devices * PARTS + (planes + 2) * GROUPS,), jnp.int32),
            pltpu.VMEM(full, F32),
            pltpu.SemaphoreType.DMA((21,)),
            pltpu.SemaphoreType.DMA((4,)),
            pltpu.SemaphoreType.DMA((8, 4)),
        ],
        compiler_params=pltpu.CompilerParams(vmem_limit_bytes=VMEM_LIMIT),
    )(*(() if more is None else (more,)), recv, *fields, *halos)


def shards(pressure, vel_inline, vel_xline, vel_depth, modulus, buoyancy, traces, owner, node_cell, resample):
    fields = (pressure, vel_inline, vel_xline, vel_depth, modulus, buoyancy)
    block = pressure.shape
    devices = lax.axis_size("xline") * lax.axis_size("inline")
    nodes = traces.shape[0]
    capacity = max(4, 5 * nodes // (2 * devices))
    most = min(nodes, 9 * capacity)
    rounds = -(-most // SLOTS)

    low_cols, high_cols, near_send, far_send = edge_pack(*fields)
    right = rotate(low_cols, "xline", -1)
    left = rotate(high_cols, "xline", 1)
    count = lax.axis_size("inline")
    near = lax.ppermute(near_send, "inline", [(source, source ^ 1) for source in range(count)])
    far = lax.ppermute(
        far_send,
        "inline",
        [(source, source if source in (0, count - 1) else ((source - 1) ^ 1) + 1) for source in range(count)],
    )

    owner_row, cell_row = owner.reshape(1, nodes), node_cell
    send = route(traces, resample, owner_row, cell_row, (0,), block)

    def exchange(packed):
        return lax.all_to_all(packed, ("xline", "inline"), split_axis=0, concat_axis=0, tiled=True)

    low_corner, high_corner = corner_pack(near, far, low_cols, high_cols, vel_inline)
    corner_r = rotate(low_corner, "xline", -1)
    corner_l = rotate(high_corner, "xline", 1)
    recv = exchange(send.reshape(devices, 8, SLOTS)).reshape(devices * 8, SLOTS)
    over = jnp.max(recv) >= FLAG / 2
    halos = (near, far, right, left, corner_r, corner_l)

    def spill():
        packed = route(traces, resample, owner_row, cell_row, tuple(range(1, rounds)), block)
        packed = packed.reshape(rounds - 1, devices, 8, SLOTS)
        more = jnp.stack([exchange(packed[turn]) for turn in range(rounds - 1)])
        return step_all(recv, more.reshape(rounds - 1, devices * 8, SLOTS), fields, halos)

    def plain():
        return step_all(recv, None, fields, halos)

    return lax.cond(over, spill, plain) if rounds > 1 else plain()


def solution(mesh):
    field = P("inline", "xline", None)
    nodes = ("xline", "inline")
    return jax.shard_map(
        shards,
        mesh=mesh,
        in_specs=(field,) * 6 + (P(nodes, None), P(nodes, None), P(nodes), P()),
        out_specs=(field,) * 4,
        check_vma=False,
    )
```

```python
import functools

import jax
import jax.numpy as jnp
from jax import lax
from jax.experimental import pallas as pl
from jax.experimental.pallas import tpu as pltpu
from jax.sharding import PartitionSpec as P

STEPS = 4
COURANT = 0.35
HALO = 4
REACH = 3
SLOTS = 128
VMEM_LIMIT = 64 * 1024 * 1024
BATCH = 8
PARTS = SLOTS // BATCH
PART_BITS = PARTS.bit_length() - 1
UNROLL = 4
GROUPS = 8
FLAG = 4096.0
F32 = jnp.float32
BF16 = jnp.bfloat16
ANY = pl.BlockSpec(memory_space=pl.ANY)
VMEM = pl.BlockSpec(memory_space=pltpu.VMEM)
SMEM = pl.BlockSpec(memory_space=pltpu.SMEM)


def rotate(value, axis, steps):
    count = lax.axis_size(axis)
    return lax.ppermute(value, axis, [(source, (source + steps) % count) for source in range(count)])


def iota(shape, dim):
    return lax.broadcasted_iota(jnp.int32, shape, dim)


def lane_before(value):
    lanes = value.ndim - 1
    return jnp.where(iota(value.shape, lanes) == 0, 0.0, pltpu.roll(value, 1, lanes))


def lane_after(value):
    lanes = value.ndim - 1
    width = value.shape[lanes]
    return jnp.where(iota(value.shape, lanes) == width - 1, 0.0, pltpu.roll(value, width - 1, lanes))


def row_before(value):
    return jnp.where(iota(value.shape, 0) == 0, 0.0, pltpu.roll(value, 1, 0))


def half_turn(tile):
    return pltpu.roll(tile, 4, 0)


def run_copies(copies):
    for copy in copies:
        copy.start()
    return copies


class Either:
    def __init__(self, choice, first, second, index, target, sem):
        self.choice = choice
        sources = [ref.at[index] if index != () else ref for ref in (first, second)]
        self.copies = [pltpu.make_async_copy(ref, target, sem) for ref in sources]

    def start(self):
        pl.when(self.choice)(self.copies[0].start)
        pl.when(jnp.logical_not(self.choice))(self.copies[1].start)

    def wait(self):
        self.copies[0].wait()


def edge_pack_kernel(
    p, vi, vx, vd, m, b, low_out, high_out, near_out, far_out,
    strips, low, high, down, up, vel, outer, col_sems, sems, out_sems,
):
    planes, columns, depth = p.shape
    col_copies = []
    for side, start in ((0, 0), (1, columns - 8)):
        for field, ref in enumerate((vi, vx, vd, p, m, b)):
            col_copies.append(
                pltpu.make_async_copy(
                    ref.at[:, pl.ds(start, 8), :], strips.at[side, field], col_sems.at[side, field]
                )
            )
    jobs = (
        (vi, 0, 3, vel.at[0, pl.ds(1, 3)]),
        (vx, 0, 3, vel.at[1, pl.ds(1, 3)]),
        (vd, 0, 3, vel.at[2, pl.ds(1, 3)]),
        (vi, planes - 4, 4, vel.at[3]),
        (vx, planes - 4, 4, vel.at[4]),
        (vd, planes - 4, 4, vel.at[5]),
        (p, 0, 3, down.at[pl.ds(0, 3)]),
        (m, 0, 3, down.at[pl.ds(6, 3)]),
        (b, 0, 3, down.at[pl.ds(9, 3)]),
        (p, planes - 3, 3, up.at[pl.ds(0, 3)]),
        (m, planes - 3, 3, up.at[pl.ds(6, 3)]),
        (b, planes - 3, 3, up.at[pl.ds(9, 3)]),
        (vi, planes - 1, 1, up.at[pl.ds(12, 1)]),
        (p, 3, 1, outer.at[pl.ds(0, 1)]),
        (p, planes - 4, 1, outer.at[pl.ds(1, 1)]),
        (b, planes - 4, 1, outer.at[pl.ds(2, 1)]),
    )
    copies = [
        pltpu.make_async_copy(ref.at[pl.ds(start, count)], target, sems.at[index])
        for index, (ref, start, count, target) in enumerate(jobs)
    ]
    run_copies(col_copies + copies)
    sub = iota((8, depth), 0)
    down[13] = jnp.zeros((columns, depth), F32)
    for copy in col_copies:
        copy.wait()

    for copy in copies[6:]:
        copy.wait()
    even = lax.axis_index("inline") % 2 == 0

    def leave(part, start, size):
        window = pl.ds(start, size)
        return run_copies(
            [
                Either(even, up, down, window, near_out.at[window], out_sems.at[part, 0]),
                Either(even, down, up, window, far_out.at[window], out_sems.at[part, 1]),
            ]
        )

    outs = leave(0, 0, 3) + leave(1, 6, 6)

    def pair(number, _):
        base = pl.multiple_of(number * 24, 8)
        shared = [[], []]
        for half in range(2):
            index = number * 2 + half
            before = jnp.maximum(index - 1, 0)
            keep = jnp.where(index > 0, 1.0, 0.0)
            for side in range(2):
                svi, svx, svd, sp, sm, sb = (strips.at[side, field] for field in range(6))
                now_p, now_m, now_b = sp[index], sm[index], sb[index]
                div = (
                    (svi[index] - keep * svi[before])
                    + (svx[index] - row_before(svx[index]))
                    + (svd[index] - lane_before(svd[index]))
                )
                flux = COURANT * now_b * (pltpu.roll(now_p, 7, 0) - now_p)
                if side == 0:
                    div = jnp.where(sub == 2, div - flux, div)
                    tile = jnp.where(
                        sub < 3, now_p, jnp.where(sub < 6, pltpu.roll(div, 3, 0), pltpu.roll(now_m, 6, 0))
                    )
                    low[pl.ds(base + half * 8, 8), :] = tile
                    rest = jnp.where(sub < 1, pltpu.roll(now_m, 6, 0), pltpu.roll(now_b, 1, 0))
                else:
                    div = jnp.where(sub == 5, div + pltpu.roll(flux, 1, 0), div)
                    tile = jnp.where(
                        sub < 3, pltpu.roll(div, 3, 0), jnp.where(sub < 5, pltpu.roll(now_m, 5, 0), now_p)
                    )
                    high[pl.ds(base + half * 8, 8), :] = tile
                    rest = jnp.where(sub < 1, pltpu.roll(now_m, 3, 0), pltpu.roll(now_b, 4, 0))
                    high[pl.ds(planes * 12 + index, 1), :] = svx[index, 7:8, :]
                shared[side].append(rest)
        for out, (even, odd) in zip((low, high), shared):
            out[pl.ds(base + 16, 8), :] = jnp.where(sub < 4, even, half_turn(odd))
        return 0

    lax.fori_loop(0, planes // 2, pair, 0, unroll=4)
    outs += run_copies(
        [
            pltpu.make_async_copy(low, low_out, out_sems.at[4, 0]),
            pltpu.make_async_copy(high, high_out, out_sems.at[4, 1]),
        ]
    )
    for copy in copies[:6]:
        copy.wait()
    last = columns - 1
    for base, out, line in ((0, down, 12), (3, up, 13)):
        for step in range(1, 4):
            div_i = vel[base, step]
            if base or step > 1:
                div_i = div_i - vel[base, step - 1]
            vx_now = vel[base + 1, step]
            vd_now = vel[base + 2, step]
            out[2 + step] = div_i + (vx_now - row_before(vx_now)) + (vd_now - lane_before(vd_now))
            out[line, step - 1 : step, :] = vel[base + 1, step, last : last + 1, :]
    down[5] = down[5] - COURANT * down[11] * (outer[0] - down[2])
    up[3] = up[3] + COURANT * outer[2] * (up[0] - outer[1])
    outs += leave(2, 3, 3) + leave(3, 12, 2)
    for copy in outs:
        copy.wait()


def edge_pack(p, vi, vx, vd, m, b):
    planes, columns, depth = p.shape
    low = (planes * 12, depth)
    high = (planes * 13, depth)
    sheets = (14, columns, depth)
    return pl.pallas_call(
        edge_pack_kernel,
        out_shape=tuple(jax.ShapeDtypeStruct(shape, F32) for shape in (low, high, sheets, sheets)),
        in_specs=[ANY] * 6,
        out_specs=(ANY,) * 4,
        scratch_shapes=[
            pltpu.VMEM((2, 6, planes, 8, depth), F32),
            pltpu.VMEM(low, F32),
            pltpu.VMEM(high, F32),
            pltpu.VMEM(sheets, F32),
            pltpu.VMEM(sheets, F32),
            pltpu.VMEM((6, 4, columns, depth), F32),
            pltpu.VMEM((3, columns, depth), F32),
            pltpu.SemaphoreType.DMA((2, 6)),
            pltpu.SemaphoreType.DMA((16,)),
            pltpu.SemaphoreType.DMA((5, 2)),
        ],
        compiler_params=pltpu.CompilerParams(vmem_limit_bytes=VMEM_LIMIT),
    )(p, vi, vx, vd, m, b)


def corner_rows(side):
    entries = []
    for z in range(2):
        for di in range(1, HALO):
            entries += [(kind, z, di, dj) for dj in range(1, HALO + 1 - di) for kind in "pb"]
            entries += [(kind, z, di, dj) for dj in range(1, HALO - di) for kind in "dm"]
            if side == 1:
                entries.append(("line", z, di, 0))
    return entries + [("first", 0, 0, dj) for dj in range(1, HALO)]


CORNER_ROWS = 48


def corner_pack_kernel(near, far, low_cols, high_cols, vi, low_out, high_out, dn, upv, row0, vi_last, sems):
    columns, depth = near.shape[1:]
    planes = vi.shape[0]
    copies = []
    even = lax.axis_index("inline") % 2 == 0
    for side, start in ((0, 0), (1, columns - 8)):
        window = pl.ds(start, 8)
        copies += [
            Either(even, near, far, (pl.ds(0, 12), window), dn.at[side], sems.at[side, 0]),
            Either(even, far, near, (pl.ds(0, 13), window), upv.at[side], sems.at[side, 1]),
            pltpu.make_async_copy(vi.at[planes - 1, window, :], vi_last.at[side], sems.at[side, 2]),
            pltpu.make_async_copy(
                (low_cols, high_cols)[side].at[pl.ds(0, 8), :], row0.at[side], sems.at[side, 3]
            ),
        ]
    lines = [
        Either(even, far, near, (13, pl.ds(0, 8)), dn.at[2, 0], sems.at[2, 0]),
        Either(even, near, far, (12, pl.ds(0, 8)), dn.at[2, 1], sems.at[2, 1]),
    ]
    run_copies(copies + lines)
    for copy in copies + lines:
        copy.wait()
    has_before = lax.axis_index("inline") > 0
    for side, out in ((0, low_out), (1, high_out)):
        out[40:48, :] = jnp.zeros((8, depth), F32)
        for row, (kind, z, di, dj) in enumerate(corner_rows(side)):
            col = dj - 1 if side == 0 else 8 - dj
            at = slice(col, col + 1)
            if kind == "first":
                place = 2 + dj if side == 0 else 3 - dj
                value = row0[side, place : place + 1, :]
                value = value - jnp.where(has_before, upv[side, 12, at, :], 0.0)
            elif kind == "line":
                line = di - 1 if z else 3 - di
                value = dn[2, z, line : line + 1, :]
            elif z:
                value = dn[side, {"p": 0, "d": 3, "m": 6, "b": 9}[kind] + di - 1, at, :]
                if kind == "d" and di == 1:
                    value = value - vi_last[side, at, :]
            else:
                value = upv[side, {"p": 3, "d": 6, "m": 9, "b": 12}[kind] - di, at, :]
            out[row : row + 1, :] = value


def corner_pack(near, far, low_cols, high_cols, vi):
    depth = near.shape[2]
    out = jax.ShapeDtypeStruct((CORNER_ROWS, depth), F32)
    return pl.pallas_call(
        corner_pack_kernel,
        out_shape=(out, out),
        in_specs=[ANY] * 5,
        out_specs=(VMEM, VMEM),
        scratch_shapes=[
            pltpu.VMEM((3, 12, 8, depth), F32),
            pltpu.VMEM((2, 13, 8, depth), F32),
            pltpu.VMEM((2, 8, depth), F32),
            pltpu.VMEM((2, 8, depth), F32),
            pltpu.SemaphoreType.DMA((3, 4)),
        ],
        compiler_params=pltpu.CompilerParams(vmem_limit_bytes=VMEM_LIMIT),
    )(near, far, low_cols, high_cols, vi)


def split3(value):
    high = value.astype(BF16)
    rest = value - high.astype(F32)
    mid = rest.astype(BF16)
    low = (rest - mid.astype(F32)).astype(BF16)
    return high, mid, low


def route_kernel(rounds, n_inline, n_xline, block, traces, resample, owner, cell, out, places):
    planes, columns, depth = block
    nodes = traces.shape[0]
    devices = n_inline * n_xline
    sources = lax.dot_general(
        resample[...],
        traces[...],
        (((1,), (1,)), ((), ())),
        precision=lax.Precision.HIGHEST,
        preferred_element_type=F32,
    )
    own, at = owner[...], cell[...].reshape(1, nodes)
    own_x, own_i = own // n_inline, own % n_inline
    at_i, at_j = at // (columns * depth), (at // depth) % columns
    target = iota((devices, 1), 0)
    rel_i = (own_i - target % n_inline) * planes + at_i
    rel_j = (own_x - target // n_inline) * columns + at_j
    off_i = jnp.maximum(jnp.maximum(-rel_i, rel_i - (planes - 1)), 0)
    off_j = jnp.maximum(jnp.maximum(-rel_j, rel_j - (columns - 1)), 0)
    member = off_i + off_j <= REACH
    member_f = jnp.where(member, 1.0, 0.0)
    earlier = jnp.where(iota((nodes, nodes), 0) < iota((nodes, nodes), 1), 1.0, 0.0).astype(BF16)
    place = jnp.dot(member_f.astype(BF16), earlier, preferred_element_type=F32)
    places[...] = jnp.where(member, place, -1.0)
    most = jnp.max(jnp.sum(member_f, axis=1, keepdims=True))
    flag = jnp.where(most > SLOTS, FLAG, 0.0)

    high, mid, low = split3(sources)
    digits = jnp.concatenate([at % 256, (at // 256) % 256, at // 65536, own + 1], 0).astype(F32).astype(BF16)
    none = jnp.zeros(digits.shape, F32).astype(BF16)
    data = jnp.concatenate([high, digits, mid, none, low, none], 0)
    slot = iota((SLOTS, nodes), 0).astype(F32)
    raised = jnp.where(iota((8, SLOTS), 0) == 4, flag, 0.0)

    def one(index, _):
        device = index % devices
        first = (index // devices + rounds[0]) * SLOTS
        row = places[pl.ds(device, 1), :] - first.astype(F32)
        chosen = jnp.where(slot == row, 1.0, 0.0).astype(BF16)
        packed = lax.dot_general(
            data, chosen, (((1,), (1,)), ((), ())), preferred_element_type=F32
        )
        out[pl.ds(pl.multiple_of(index * 8, 8), 8), :] = (
            packed[0:8] + packed[8:16] + packed[16:24] + raised
        )
        return 0

    lax.fori_loop(0, len(rounds) * devices, one, 0, unroll=16)


def route(traces, resample, owner, cell, rounds, block):
    n_inline, n_xline = lax.axis_size("inline"), lax.axis_size("xline")
    devices = n_inline * n_xline
    nodes = traces.shape[0]
    return pl.pallas_call(
        functools.partial(route_kernel, rounds, n_inline, n_xline, block),
        out_shape=jax.ShapeDtypeStruct((len(rounds) * devices * 8, SLOTS), F32),
        in_specs=[VMEM] * 4,
        out_specs=VMEM,
        scratch_shapes=[pltpu.VMEM((devices, nodes), F32)],
        compiler_params=pltpu.CompilerParams(vmem_limit_bytes=VMEM_LIMIT),
    )(traces, resample, owner, cell)


def step_kernel(
    rounds, n_inline, n_xline, *refs
):
    if rounds:
        more, *refs = refs
    (recv, p, vi, vx, vd, m, b, near, far, right, left, corner_r, corner_l,
    p_out, vi_out, vx_out, vd_out,
    pb, div, mb, bb, inj, v0, v1, v2, p4, bs, lines, strip_r, strip_l, cor_r, cor_l,
    lists, codes_v, later_v, parity, counts_v, codes, late_codes, counts, batches, bk, sems, list_sems, out_sems) = refs
    planes, columns, depth = p.shape
    rows = columns + 8
    devices = n_inline * n_xline
    at_i, at_x = lax.axis_index("inline"), lax.axis_index("xline")
    own_p, own_c = pl.ds(4, planes), pl.ds(0, columns)
    lane_tiles = depth // 128
    inj_planes = planes + 2 * REACH
    dummy = lane_tiles * inj_planes * rows // 2

    nothing = devices * PARTS
    arrived = lists.at[pl.ds(0, devices * 8), :]
    lists[pl.ds(devices * 8, 8), :] = jnp.zeros((8, SLOTS), F32)
    first_list = pltpu.make_async_copy(recv, arrived, list_sems.at[0])
    first_list.start()
    jobs = (
        (vi, v0.at[pl.ds(1, planes)]),
        (vx, v1),
        (vd, v2),
        (b, bb.at[own_p, own_c, :]),
        (right, strip_r),
        (left, strip_l),
        (p, pb.at[0, own_p, own_c, :]),
        (m, mb.at[own_p, own_c, :]),
        (corner_r, cor_r),
        (corner_l, cor_l),
    )
    up_jobs = (
        (pl.ds(0, 3), pb.at[0, pl.ds(1, 3), own_c, :]),
        (pl.ds(3, 3), div.at[pl.ds(1, 3), own_c, :]),
        (pl.ds(6, 3), mb.at[pl.ds(1, 3), own_c, :]),
        (pl.ds(9, 3), bb.at[pl.ds(1, 3), own_c, :]),
        (12, v0.at[0]),
        ((13, pl.ds(0, 8)), lines.at[0]),
    )
    down_jobs = (
        (pl.ds(0, 3), pb.at[0, pl.ds(planes + 4, 3), own_c, :]),
        (pl.ds(3, 3), div.at[pl.ds(planes + 4, 3), own_c, :]),
        (pl.ds(6, 3), mb.at[pl.ds(planes + 4, 3), own_c, :]),
        (pl.ds(9, 3), bb.at[pl.ds(planes + 4, 3), own_c, :]),
        ((12, pl.ds(0, 8)), lines.at[1]),
    )
    even = at_i % 2 == 0
    copies = [pltpu.make_async_copy(src, dst, sems.at[index]) for index, (src, dst) in enumerate(jobs)]
    ups = [
        Either(even, far, near, index, dst, sems.at[10 + job]) for job, (index, dst) in enumerate(up_jobs)
    ]
    downs = [
        Either(even, near, far, index, dst, sems.at[16 + job]) for job, (index, dst) in enumerate(down_jobs)
    ]
    early = run_copies(copies[:6] + [ups[4]])
    late = copies[6:] + ups[:4] + ups[5:] + downs

    def clear(index, _):
        inj[pl.ds(pl.multiple_of(index * rows * STEPS, 8), rows * STEPS), :] = jnp.zeros(
            (rows * STEPS, 128), F32
        )
        return 0

    lax.fori_loop(0, lane_tiles * inj_planes, clear, 0)
    first_list.wait()
    sub = iota((8, SLOTS), 0)
    lane = iota((8, SLOTS), 1)

    low_i, high_i = at_i == 0, at_i == n_inline - 1
    low_x, high_x = at_x == 0, at_x == n_xline - 1
    keep_x = jnp.where(low_x, 0.0, 1.0)
    end_x = jnp.where(high_x, 0.0, 1.0)
    top = iota((8, depth), 0) == 0
    top_own = iota((columns, depth), 0) == 0
    edge = slice(columns, columns + 8)
    sub_d = iota((8, depth), 0)
    upper = sub_d >= 4
    square = COURANT * COURANT

    def own_plane(index):
        plane = index + 4
        pair, odd = index // 2, index % 2
        tile_at = pl.ds(pl.multiple_of(pair * 24 + odd * 8, 8), 8)
        rest_at = pl.ds(pl.multiple_of(pair * 24 + 16, 8), 8)
        t_l, t_r = strip_l[tile_at, :], strip_r[tile_at, :]
        rest_l, rest_r = strip_l[rest_at, :], strip_r[rest_at, :]
        rest_l = jnp.where(odd == 1, half_turn(rest_l), rest_l)
        rest_r = jnp.where(odd == 1, half_turn(rest_r), rest_r)
        vx_l = keep_x * strip_l[pl.ds(planes * 12 + index, 1), :]
        now_x, now_d = v1[index], v2[index]
        p_l = jnp.where(sub_d == 4, pltpu.roll(t_l, 7, 0), t_l)
        p_r = jnp.where(sub_d == 3, pltpu.roll(t_r, 1, 0), t_r)
        pb[0, plane, edge, :] = jnp.where(upper, p_l, end_x * p_r)
        m_l = jnp.where(sub_d == 5, pltpu.roll(rest_l, 5, 0), pltpu.roll(t_l, 3, 0))
        m_r = jnp.where(sub_d == 2, pltpu.roll(rest_r, 2, 0), pltpu.roll(t_r, 2, 0))
        mb[plane, edge, :] = jnp.where(upper, m_l, end_x * m_r)
        turned = pltpu.roll(jnp.where((sub_d >= 3) & (sub_d < 6), t_r, t_l), 5, 0)
        div[plane, edge, :] = COURANT * (turned - jnp.where(top, now_x[columns - 1 : columns, :], 0.0))
        buoy = square * jnp.where(upper, keep_x * half_turn(rest_l), pltpu.roll(rest_r, 7, 0))
        bs[plane, edge, :] = buoy
        bk[plane, edge, :] = lane_before(buoy)
        x_before = jnp.where(top_own, vx_l, pltpu.roll(now_x, 1, 0))
        div[plane, own_c, :] = COURANT * (
            (v0[index + 1] - v0[index]) + (now_x - x_before) + (now_d - lane_before(now_d))
        )
        buoy = square * bb[plane, own_c, :]
        bs[plane, own_c, :] = buoy
        bk[plane, own_c, :] = lane_before(buoy)

    def start_block():
        for copy in early:
            copy.wait()
        run_copies(late)

        @pl.when(low_i)
        def _():
            v0[0] = jnp.zeros((columns, depth), F32)

    def one_round(turn, _):
        if rounds:
            @pl.when(turn > 0)
            def _():
                copy = pltpu.make_async_copy(more.at[jnp.maximum(turn - 1, 0)], arrived, list_sems.at[0])
                copy.start()
                copy.wait()

        digit0 = lists[pl.ds(4, devices, stride=8), :]
        digit0 = digit0 - jnp.where(digit0 >= FLAG, FLAG, 0.0)
        digit1 = lists[pl.ds(5, devices, stride=8), :]
        digit2 = lists[pl.ds(6, devices, stride=8), :]
        named = lists[pl.ds(7, devices, stride=8), :]
        cell = (digit0 + 256.0 * digit1 + 65536.0 * digit2).astype(jnp.int32)
        own = jnp.maximum(named.astype(jnp.int32) - 1, 0)
        rel_i = (own % n_inline - at_i) * planes + cell // (columns * depth)
        rel_j = (own // n_inline - at_x) * columns + (cell // depth) % columns
        k = cell % depth
        flat = (rel_i + REACH) * rows + jnp.where(rel_j < 0, rel_j + rows, rel_j)
        tile = (k // 128) * (inj_planes * rows // 2) + flat // 2
        slot = iota(tile.shape, 1)
        code = tile * SLOTS + ((k - slot) & (SLOTS - 1))
        parity[...] = flat % 2
        valid = named > 0.0
        tile = jnp.where(valid, tile, -1)
        clash = jnp.zeros(tile.shape, jnp.int32)
        for back in range(1, BATCH):
            same = (pltpu.roll(tile, back, 1) == tile) & (slot % BATCH >= back)
            clash = jnp.where(same, 1, clash)
        now = valid & (clash == 0)
        later = valid & (clash == 1)
        codes_v[0:devices, :] = jnp.where(now, code, dummy * SLOTS)
        codes_v[devices:, :] = jnp.full((8, SLOTS), dummy * SLOTS, jnp.int32)
        later_v[...] = jnp.where(later, code, dummy * SLOTS)
        count = jnp.sum(jnp.where(valid, 1.0, 0.0), axis=1, keepdims=True).astype(jnp.int32)
        put_off = jnp.where(later, 1, 0)
        for ahead in (4, 2, 1):
            put_off = jnp.maximum(put_off, pltpu.roll(put_off, SLOTS - ahead, 1))
        any_off = jnp.max(put_off.astype(F32), axis=1, keepdims=True).astype(jnp.int32)
        counts_v[...] = jnp.where(
            slot % BATCH == 0, put_off, jnp.where(slot == 1, count, any_off)
        )
        to_smem = run_copies(
            [
                pltpu.make_async_copy(codes_v, codes, list_sems.at[1]),
                pltpu.make_async_copy(counts_v, counts, list_sems.at[2]),
                pltpu.make_async_copy(later_v, late_codes, list_sems.at[3]),
            ]
        )
        for copy in to_smem:
            copy.wait()

        def one_list(source, total):
            rows8 = pl.ds(pl.multiple_of(source * 8, 8), 8)
            tile8 = lists[rows8, :]
            odd = jnp.broadcast_to(parity[pl.ds(source, 1), :], (8, SLOTS))
            mine = jnp.where(sub < 4, tile8, half_turn(tile8))
            lists[rows8, :] = jnp.where(sub // 4 == odd, COURANT * mine, 0.0)
            for part in range(PARTS):
                batches[total + part] = source * PARTS + part
            return total + (counts[source, 1] + BATCH - 1) // BATCH

        total = lax.fori_loop(0, devices, one_list, 0, unroll=4)

        def pad(index, _):
            for extra in range(GROUPS):
                batches[total + index * GROUPS + extra] = nothing
            return 0

        lax.fori_loop(0, jnp.maximum(planes - total // GROUPS, 1), pad, 0)

        def spread(values, code, slot_at):
            alone = jnp.where(lane == slot_at, values, 0.0)
            return pltpu.roll(alone, code & (SLOTS - 1), 1)

        def prepare(index):
            name = batches[index]
            source, base = name >> PART_BITS, (name & (PARTS - 1)) * BATCH
            values = lists[pl.ds(pl.multiple_of(source * 8, 8), 8), :]
            found = [codes[source, base + unit] for unit in range(BATCH)]
            rows_at = [pl.ds(pl.multiple_of((code >> 7) * 8, 8), 8) for code in found]
            return [spread(values, code, base + unit) for unit, code in enumerate(found)], rows_at

        def add_groups(index):
            ready = [prepare(index * GROUPS + group) for group in range(GROUPS)]
            for adds, rows_at in ready:
                sums = [inj[row, :] + add for row, add in zip(rows_at, adds)]
                for row, value in zip(rows_at, sums):
                    inj[row, :] = value

        def both(index, _):
            add_groups(index)
            own_plane(index)
            return 0

        def batch(index, _):
            add_groups(index)
            return 0

        if not rounds:
            start_block()
        turns = jnp.maximum((total + GROUPS - 1) // GROUPS, planes)
        lax.fori_loop(0, planes, both, 0)
        lax.fori_loop(planes, turns, batch, 0)

        def put_off_list(source, _):
            @pl.when(counts[source, 2] > 0)
            def _():
                values = lists[pl.ds(pl.multiple_of(source * 8, 8), 8), :]

                def part_of(part, _):
                    @pl.when(counts[source, part * BATCH] > 0)
                    def _():
                        for unit in range(BATCH):
                            slot_at = part * BATCH + unit
                            code = late_codes[source, slot_at]
                            row = pl.ds(pl.multiple_of((code >> 7) * 8, 8), 8)
                            inj[row, :] += spread(values, code, slot_at)

                    return 0

                lax.fori_loop(0, PARTS, part_of, 0)

            return 0

        lax.fori_loop(0, devices, put_off_list, 0)
        return 0

    if rounds:
        start_block()
        lax.fori_loop(0, 1 + rounds, one_round, 0)
    else:
        one_round(0, 0)
    for copy in late:
        copy.wait()

    bb[0] = jnp.zeros((rows, depth), F32)
    pb[0, 0, own_c, :] = pb[0, 1, own_c, :]
    pb[0, planes + 7, own_c, :] = pb[0, planes + 6, own_c, :]
    own_line = v1[0, columns - 1 : columns, :]
    for side, box in ((0, cor_r), (1, cor_l)):
        for row, (kind, z, di, dj) in enumerate(corner_rows(side)):
            plane = planes + 3 + di if z else 4 - di
            spot = columns + dj - 1 if side == 0 else rows - dj
            at = slice(spot, spot + 1)
            value = box[row : row + 1, :]
            line = di - 1 if z else 3 - di
            if kind == "p":
                pb[0, plane, at, :] = value
            elif kind == "b":
                bb[plane, at, :] = value
            elif kind == "m":
                mb[plane, at, :] = value
            elif kind == "line":
                fix = jnp.where(top_own, keep_x * value, 0.0)
                if z and di == 1:
                    fix = fix + v0[planes]
                div[plane, own_c, :] = COURANT * (div[plane, own_c, :] - fix)
            else:
                if side == 0 and dj == 1:
                    value = value - (own_line if kind == "first" else lines[z, line : line + 1, :])
                div[plane, at, :] = COURANT * value

    for first in (0, planes + 4):
        @pl.when(low_x)
        def _(first=first):
            bb[first : first + 4, columns + 4 :, :] = jnp.zeros((4, 4, depth), F32)

        @pl.when(high_x)
        def _(first=first):
            pb[0, first : first + 4, columns : columns + 4, :] = jnp.zeros((4, 4, depth), F32)
            mb[first : first + 4, columns : columns + 4, :] = jnp.zeros((4, 4, depth), F32)

    @pl.when(low_i)
    def _():
        bb[0:4] = jnp.zeros((4, rows, depth), F32)

    @pl.when(high_i)
    def _():
        pb[0, planes + 4 :] = jnp.zeros((4, rows, depth), F32)
        mb[planes + 4 :] = jnp.zeros((4, rows, depth), F32)

    for plane in (0, 1, 2, 3, planes + 4, planes + 5, planes + 6):
        buoy = square * bb[plane]
        bs[plane] = buoy
        bk[plane] = lane_before(buoy)

    def advance(step, plane, flux_before):
        now, after, buoy = pb[step, plane], pb[step, plane + 1], bs[plane]
        flux_i = buoy * (after - now)
        flux_x = buoy * (pltpu.roll(now, rows - 1, 0) - now)
        change_d = buoy * (lane_after(now) - now) - bk[plane] * (now - pltpu.roll(now, 1, 1))
        change = (
            (flux_i - flux_before)
            + (flux_x - pltpu.roll(flux_x, 1, 0))
            + change_d
        )
        new_div = div[plane] - change
        source = jnp.concatenate(
            [
                inj[pl.ds((part * inj_planes + plane - 1) * rows * STEPS + step, rows, stride=STEPS), :]
                for part in range(lane_tiles)
            ],
            1,
        )
        return flux_i, new_div, now - mb[plane] * (new_div - source)

    for step in range(STEPS - 1):
        def one_plane(plane, flux_before, step=step):
            flux_i, new_div, new_p = advance(step, plane, flux_before)
            div[plane] = new_div
            pb[step + 1, plane] = new_p
            return flux_i

        start = 1 + step
        flux = bs[step] * (pb[step, start] - pb[step, step])
        lax.fori_loop(start, planes + 7 - step, one_plane, flux, unroll=UNROLL)

    last = STEPS - 1

    def total(plane):
        return (pb[0, plane] + pb[1, plane]) + (pb[2, plane] + pb[3, plane])

    def last_plane(index, flux_before):
        plane = index + 4
        flux_i, _, new_p = advance(last, plane, flux_before)
        p4[index] = new_p[:columns]
        here, there = total(plane), total(plane + 1)
        scaled = (1.0 / COURANT) * bs[plane, own_c, :]
        mine = here[:columns]
        v0[index + 1] = v0[index + 1] - scaled * (there[:columns] - mine)
        v1[index] = v1[index] - scaled * (pltpu.roll(here, rows - 1, 0)[:columns] - mine)
        v2[index] = v2[index] - scaled * (lane_after(mine) - mine)
        return flux_i

    flux = bs[3] * (pb[last, 4] - pb[last, 3])
    chunk = planes // 8
    outs = []
    for part in range(8):
        flux = lax.fori_loop(part * chunk, (part + 1) * chunk, last_plane, flux, unroll=UNROLL)
        window = pl.ds(part * chunk, chunk)
        outs += run_copies(
            [
                pltpu.make_async_copy(src, dst.at[window], out_sems.at[part, index])
                for index, (src, dst) in enumerate(
                    (
                        (p4.at[window], p_out),
                        (v0.at[pl.ds(part * chunk + 1, chunk)], vi_out),
                        (v1.at[window], vx_out),
                        (v2.at[window], vd_out),
                    )
                )
            ]
        )
    for copy in outs:
        copy.wait()


def step_all(recv, more, fields, halos):
    p = fields[0]
    planes, columns, depth = p.shape
    n_inline, n_xline = lax.axis_size("inline"), lax.axis_size("xline")
    devices = n_inline * n_xline
    rows = columns + 8
    full = (planes + 8, rows, depth)
    block = (planes, columns, depth)
    inj_rows = (depth // 128) * (planes + 2 * REACH) * rows * STEPS
    return pl.pallas_call(
        functools.partial(step_kernel, 0 if more is None else more.shape[0], n_inline, n_xline),
        out_shape=tuple(jax.ShapeDtypeStruct(block, F32) for _ in range(4)),
        in_specs=[ANY] * (13 if more is None else 14),
        out_specs=(ANY,) * 4,
        scratch_shapes=[
            pltpu.VMEM((STEPS,) + full, F32),
            pltpu.VMEM(full, F32),
            pltpu.VMEM(full, F32),
            pltpu.VMEM(full, F32),
            pltpu.VMEM((inj_rows + 8, 128), F32),
            pltpu.VMEM((planes + 1, columns, depth), F32),
            pltpu.VMEM(block, F32),
            pltpu.VMEM(block, F32),
            pltpu.VMEM(block, F32),
            pltpu.VMEM(full, F32),
            pltpu.VMEM((2, 8, depth), F32),
            pltpu.VMEM((planes * 12, depth), F32),
            pltpu.VMEM((planes * 13, depth), F32),
            pltpu.VMEM((CORNER_ROWS, depth), F32),
            pltpu.VMEM((CORNER_ROWS, depth), F32),
            pltpu.VMEM((devices * 8 + 8, SLOTS), F32),
            pltpu.VMEM((devices + 8, SLOTS), jnp.int32),
            pltpu.VMEM((devices, SLOTS), jnp.int32),
            pltpu.VMEM((devices, SLOTS), jnp.int32),
            pltpu.VMEM((devices, SLOTS), jnp.int32),
            pltpu.SMEM((devices + 8, SLOTS), jnp.int32),
            pltpu.SMEM((devices, SLOTS), jnp.int32),
            pltpu.SMEM((devices, SLOTS), jnp.int32),
            pltpu.SMEM((devices * PARTS + (planes + 2) * GROUPS,), jnp.int32),
            pltpu.VMEM(full, F32),
            pltpu.SemaphoreType.DMA((21,)),
            pltpu.SemaphoreType.DMA((4,)),
            pltpu.SemaphoreType.DMA((8, 4)),
        ],
        compiler_params=pltpu.CompilerParams(vmem_limit_bytes=VMEM_LIMIT),
    )(*(() if more is None else (more,)), recv, *fields, *halos)


def shards(pressure, vel_inline, vel_xline, vel_depth, modulus, buoyancy, traces, owner, node_cell, resample):
    fields = (pressure, vel_inline, vel_xline, vel_depth, modulus, buoyancy)
    block = pressure.shape
    devices = lax.axis_size("xline") * lax.axis_size("inline")
    nodes = traces.shape[0]
    capacity = max(4, 5 * nodes // (2 * devices))
    most = min(nodes, 9 * capacity)
    rounds = -(-most // SLOTS)

    low_cols, high_cols, near_send, far_send = edge_pack(*fields)
    right = rotate(low_cols, "xline", -1)
    left = rotate(high_cols, "xline", 1)
    count = lax.axis_size("inline")
    near = lax.ppermute(near_send, "inline", [(source, source ^ 1) for source in range(count)])
    far = lax.ppermute(
        far_send,
        "inline",
        [(source, source if source in (0, count - 1) else ((source - 1) ^ 1) + 1) for source in range(count)],
    )

    owner_row, cell_row = owner.reshape(1, nodes), node_cell
    send = route(traces, resample, owner_row, cell_row, (0,), block)

    def exchange(packed):
        return lax.all_to_all(packed, ("xline", "inline"), split_axis=0, concat_axis=0, tiled=True)

    low_corner, high_corner = corner_pack(near, far, low_cols, high_cols, vel_inline)
    corner_r = rotate(low_corner, "xline", -1)
    corner_l = rotate(high_corner, "xline", 1)
    recv = exchange(send.reshape(devices, 8, SLOTS)).reshape(devices * 8, SLOTS)
    over = jnp.max(recv) >= FLAG / 2
    halos = (near, far, right, left, corner_r, corner_l)

    def spill():
        packed = route(traces, resample, owner_row, cell_row, tuple(range(1, rounds)), block)
        packed = packed.reshape(rounds - 1, devices, 8, SLOTS)
        more = jnp.stack([exchange(packed[turn]) for turn in range(rounds - 1)])
        return step_all(recv, more.reshape(rounds - 1, devices * 8, SLOTS), fields, halos)

    def plain():
        return step_all(recv, None, fields, halos)

    return lax.cond(over, spill, plain) if rounds > 1 else plain()


def solution(mesh):
    field = P("inline", "xline", None)
    nodes = ("xline", "inline")
    return jax.shard_map(
        shards,
        mesh=mesh,
        in_specs=(field,) * 6 + (P(nodes, None), P(nodes, None), P(nodes), P()),
        out_specs=(field,) * 4,
        check_vma=False,
    )
```
